32 devices in a mesh: blk: 4 (over x, core), tensor: 8 (over z, y).
Axes of the slice: x: 2, y: 2, z: 4, core: 2. Of those that a mesh axis runs over, the one named last changes fastest.
Arguments:
- hidden_in: bfloat16 [4, 1024, 2048], P(None, 'blk'), may hold values from -6 to 6
- out_grad: bfloat16 [4, 1024, 2048], P(None, 'blk'), may hold values from -6 to 6
- norm_in: bfloat16 [2048], P('blk'), may hold values from 0.5 to 1.5
- w_query: bfloat16 [2048, 2048], P('blk', 'tensor'), may hold values from -0.125 to 0.125
- key_weight: bfloat16 [2048, 1024], P('blk', 'tensor'), may hold values from -0.125 to 0.125
- value_weight: bfloat16 [2048, 1024], P('blk', 'tensor'), may hold values from -0.125 to 0.125
- w_out: bfloat16 [2048, 2048], P('tensor', 'blk'), may hold values from -1 to 1
- query_gain: bfloat16 [128], P('blk'), may hold values from 0.5 to 1.5
- key_gain: bfloat16 [128], P('blk'), may hold values from 0.5 to 1.5
- norm_mid: bfloat16 [2048], P('blk'), may hold values from 0.5 to 1.5
- w_gate: bfloat16 [2048, 6144], P('blk', 'tensor'), may hold values from -0.125 to 0.125
- w_up: bfloat16 [2048, 6144], P('blk', 'tensor'), may hold values from -0.125 to 0.125
- w_down: bfloat16 [6144, 2048], P('tensor', 'blk'), may hold values from -0.078125 to 0.078125
Outputs:
- layer_out: bfloat16 [4, 1024, 2048], P(None, 'blk')
- grad_hidden: bfloat16 [4, 1024, 2048], P(None, 'blk')
- grad_norm_in: float32 [2048], P('blk')
- grad_w_query: float32 [2048, 2048], P('blk', 'tensor')
- grad_w_key: float32 [2048, 1024], P('blk', 'tensor')
- grad_w_value: float32 [2048, 1024], P('blk', 'tensor')
- grad_w_out: float32 [2048, 2048], P('tensor', 'blk')
- grad_query_gain: float32 [128], P('blk')
- grad_key_gain: float32 [128], P('blk')
- grad_norm_mid: float32 [2048], P('blk')
- grad_w_gate: float32 [2048, 6144], P('blk', 'tensor')
- grad_w_up: float32 [2048, 6144], P('blk', 'tensor')
- grad_w_down: float32 [6144, 2048], P('tensor', 'blk')
The draws below stay inside these ranges and needn't reach their ends.
All inputs are finite; a program needn't handle non-finite values.
Results may differ from the reference program's by a relative error of at most 0.025.
Values may be sent and summed in bfloat16 or wider, within the bound.
No kernel may reach another device: no remote copies, remote signals or barrier semaphores. Data moves between devices by JAX's collectives and lax.ppermute only.
A program may use at most 192 MiB of HBM per device.

```python
import math
import jax
import jax.numpy as jnp
from jax import lax

MODEL_WIDTH = 2048
HQ = 16
KEY_VALUE_HEADS = 8
HEAD_SIZE = 128
FF = 6144
MB = 4
SEQ = 1024


def block_levels(key, dims, cuts, smallest, largest):
    factor_of = 1.0
    for dim, blocks in cuts:
        heights = jax.random.uniform(jax.random.fold_in(jax.random.fold_in(key, 6), dim), (blocks,), jnp.float32, smallest / len(cuts), largest / len(cuts))
        factor_of = factor_of * jnp.repeat(jnp.exp(heights), dims[dim] // blocks).reshape((-1,) + (1,) * (len(dims) - 1 - dim))
    return factor_of


def normal_values(key, extent, deviation, reach, pieces=(), kind=jnp.bfloat16):
    values = jax.random.normal(key, extent, jnp.float32) * deviation
    if len(pieces) > 0:
        values = block_levels(key, extent, pieces, -0.22, 0.18) * values
    return jnp.clip(values, min=-reach, max=reach).astype(kind)


def setup_inputs(seed: int = 0) -> dict:
    streams_of = jax.random.split(jax.random.key(seed), 14)
    return {
        "hidden_in": normal_values(streams_of[0], (MB, SEQ, MODEL_WIDTH), 1.0, 6.0, ((1, 4),)),
        "out_grad": normal_values(streams_of[1], (MB, SEQ, MODEL_WIDTH), 1.0, 6.0, ((1, 4),)),
        "norm_in": jnp.clip(1.0 + 0.1 * jax.random.normal(streams_of[2], (MODEL_WIDTH,), jnp.float32), 0.5, 1.5).astype(jnp.bfloat16),
        "w_query": normal_values(streams_of[3], (MODEL_WIDTH, HQ * HEAD_SIZE), MODEL_WIDTH ** -0.5, 0.125, ((0, 4), (1, 8))),
        "key_weight": normal_values(streams_of[4], (MODEL_WIDTH, KEY_VALUE_HEADS * HEAD_SIZE), MODEL_WIDTH ** -0.5, 0.125, ((0, 4), (1, 8))),
        "value_weight": normal_values(streams_of[5], (MODEL_WIDTH, KEY_VALUE_HEADS * HEAD_SIZE), MODEL_WIDTH ** -0.5, 0.125, ((0, 4), (1, 8))),
        "w_out": normal_values(streams_of[6], (HQ * HEAD_SIZE, MODEL_WIDTH), (max(1, HQ * HEAD_SIZE * 16 // SEQ)) ** -0.5, 1.0, ((0, 8), (1, 4))),
        "query_gain": jnp.clip(1.0 + 0.1 * jax.random.normal(streams_of[7], (HEAD_SIZE,), jnp.float32), 0.5, 1.5).astype(jnp.bfloat16),
        "key_gain": jnp.clip(1.0 + 0.1 * jax.random.normal(streams_of[8], (HEAD_SIZE,), jnp.float32), 0.5, 1.5).astype(jnp.bfloat16),
        "norm_mid": jnp.clip(1.0 + 0.1 * jax.random.normal(streams_of[9], (MODEL_WIDTH,), jnp.float32), 0.5, 1.5).astype(jnp.bfloat16),
        "w_gate": normal_values(streams_of[10], (MODEL_WIDTH, FF), MODEL_WIDTH ** -0.5, 0.125, ((0, 4), (1, 8))),
        "w_up": normal_values(streams_of[11], (MODEL_WIDTH, FF), MODEL_WIDTH ** -0.5, 0.125, ((0, 4), (1, 8))),
        "w_down": normal_values(streams_of[12], (FF, MODEL_WIDTH), FF ** -0.5, 0.078125, ((0, 8), (1, 4))),
    }


EPSILON = 1e-06
ROTARY_BASE = 1000000.0
HIGHEST = lax.Precision.HIGHEST

@jax.custom_vjp
def low(v):
    return lax.optimization_barrier(v.astype(jnp.bfloat16)).astype(jnp.float32)

@jax.custom_vjp
def low_back(v):
    return v

def low_keep(v):
    return (low(v), None)

def low_pass(kept, grad):
    return (grad,)

def back_keep(v):
    return (v, None)

def back_low(kept, grad):
    return (low(grad),)
low.defvjp(low_keep, low_pass)
low_back.defvjp(back_keep, back_low)

def normed(values, row_gain_vector):
    return values * lax.rsqrt(lax.optimization_barrier(jnp.mean(values * values, axis=-1, keepdims=True)) + EPSILON) * row_gain_vector

def rotate(values, cosine, sine_table):
    half_dim = values.shape[-1] // 2
    first_half = values[..., :half_dim]
    second_half = values[..., half_dim:]
    return jnp.concatenate([first_half * cosine - second_half * sine_table, second_half * cosine + first_half * sine_table], axis=-1)

def rotation_tables(positions, head_dim):
    half_dim = head_dim // 2
    inverse = jnp.power(jnp.float32(ROTARY_BASE), -(jnp.arange(half_dim, dtype=jnp.float32) * 2.0 / head_dim))
    angles = positions.astype(jnp.float32)[:, None] * inverse[None, :]
    return (jnp.cos(angles)[:, None, :], jnp.sin(angles)[:, None, :])

def product(left_side, right_side):
    return jnp.dot(left_side, right_side, precision=HIGHEST)

def attention(query_rows, key_rows, value_rows):
    length, head_count, head_dim = query_rows.shape
    group_size = head_count // key_rows.shape[1]
    key_full = jnp.repeat(key_rows, group_size, axis=1)
    value_full = jnp.repeat(value_rows, group_size, axis=1)
    rows_block = math.gcd(length, 512)
    score_scale = head_dim ** (-0.5)
    key_positions = jnp.arange(length, dtype=jnp.int32)

    def score_block(query_block, first_row):
        scores = low_back(jnp.einsum('qhd,khd->hqk', query_block, key_full, precision=HIGHEST)) * score_scale
        query_positions = first_row + jnp.arange(rows_block, dtype=jnp.int32)
        scores = jnp.where(key_positions[None, None, :] <= query_positions[None, :, None], scores, -jnp.inf)
        row_max = lax.optimization_barrier(jnp.max(scores, axis=-1, keepdims=True))
        exponents = jnp.exp(scores - row_max)
        probabilities = exponents / lax.optimization_barrier(jnp.sum(exponents, axis=-1, keepdims=True))
        return jnp.einsum('hqk,khd->qhd', low(probabilities), value_full, precision=HIGHEST)
    checked = jax.checkpoint(score_block)

    def run_block(pair_in):
        return checked(pair_in[0], pair_in[1])
    blocks_in = query_rows.reshape(length // rows_block, rows_block, head_count, head_dim)
    firsts = jnp.arange(length // rows_block, dtype=jnp.int32) * rows_block
    outputs = lax.map(run_block, (blocks_in, firsts))
    return outputs.reshape(length, head_count * head_dim)

def decoder_layer(x_rows, norm_in, w_query, key_weight, value_weight, w_out, query_gain, key_gain, norm_mid, w_gate, w_up, w_down):
    length = x_rows.shape[0]
    head_dim = query_gain.shape[0]
    cosine, sine_table = rotation_tables(jnp.arange(length, dtype=jnp.int32), head_dim)
    normal_in = low(normed(x_rows, norm_in))
    query_raw = low_back(product(normal_in, w_query)).reshape(length, -1, head_dim)
    key_raw = low_back(product(normal_in, key_weight)).reshape(length, -1, head_dim)
    value_rows = low(low_back(product(normal_in, value_weight))).reshape(length, -1, head_dim)
    query_rows = low(rotate(normed(query_raw, query_gain), cosine, sine_table))
    key_rows = low(rotate(normed(key_raw, key_gain), cosine, sine_table))
    attended = low(low_back(attention(query_rows, key_rows, value_rows)))
    residual = x_rows + low_back(product(attended, w_out))
    normal_mid = low(normed(residual, norm_mid))
    gate_rows = low_back(product(normal_mid, w_gate))
    up_rows = low_back(product(normal_mid, w_up))
    active = low(jax.nn.silu(gate_rows) * up_rows)
    return residual + low_back(product(active, w_down))

def reference(hidden_in, out_grad, norm_in, w_query, key_weight, value_weight, w_out, query_gain, key_gain, norm_mid, w_gate, w_up, w_down):
    weights = tuple((argument.astype(jnp.float32) for argument in (norm_in, w_query, key_weight, value_weight, w_out, query_gain, key_gain, norm_mid, w_gate, w_up, w_down)))

    def one_sequence(totals, inputs):
        x_rows, grad_rows = inputs
        result, pullback = jax.vjp(decoder_layer, x_rows.astype(jnp.float32), *weights)
        gradients = pullback(grad_rows.astype(jnp.float32))
        totals = tuple((running + gradient for running, gradient in zip(totals, gradients[1:])))
        return (totals, (result.astype(jnp.bfloat16), gradients[0].astype(jnp.bfloat16)))
    initial = tuple((jnp.zeros(argument.shape, jnp.float32) for argument in weights))
    totals, (layer_out, grad_hidden) = lax.scan(one_sequence, initial, (hidden_in, out_grad))
    return (layer_out, grad_hidden, totals[0], totals[1], totals[2], totals[3], totals[4], totals[5], totals[6], totals[7], totals[8], totals[9], totals[10])
```

```python
import jax
import jax.numpy as jnp
from jax import lax
from jax.sharding import Mesh
from jax.sharding import PartitionSpec as P

EPSILON = 1e-06
ROTARY_BASE = 1000000.0
BF16 = jnp.bfloat16
F32 = jnp.float32
BLOCKS = ("bo", "bi")
TENSORS = ("to", "ti")


def normed(values, gain):
    return values * lax.rsqrt(jnp.mean(values * values, axis=-1, keepdims=True) + EPSILON) * gain


def rotate(values, cosine, sine):
    half = values.shape[-1] // 2
    first = values[..., :half]
    second = values[..., half:]
    return jnp.concatenate(
        [first * cosine - second * sine, second * cosine + first * sine], axis=-1
    )


def rotation_tables(positions, head_dim):
    half = head_dim // 2
    inverse = jnp.power(F32(ROTARY_BASE), -(jnp.arange(half, dtype=F32) * 2.0 / head_dim))
    angles = positions.astype(F32)[:, None] * inverse[None, :]
    return (jnp.cos(angles)[:, None, :], jnp.sin(angles)[:, None, :])


def dot(left, right):
    return jnp.dot(left, right, preferred_element_type=F32)


def dot_back(left, right):
    return jnp.einsum("tc,dc->td", left, right, preferred_element_type=F32)


def after(array, *earlier):
    return lax.optimization_barrier((array,) + earlier)[0]


def shifted(array, axis, step):
    count = lax.axis_size(axis)
    return lax.ppermute(array, axis, [(i, (i + step) % count) for i in range(count)])


def swapped(array, axis, distance=1):
    count = lax.axis_size(axis)
    return lax.ppermute(array, axis, [(i, i ^ distance) for i in range(count)])


def pick(array, index, dimension=0):
    return lax.dynamic_index_in_dim(array, index, dimension, keepdims=False)


def paired(own, other, first, dimension):
    return jnp.where(
        first, jnp.stack([own, other], dimension), jnp.stack([other, own], dimension)
    )


def gather_axis(array, axis, dimension=0):
    count = lax.axis_size(axis)
    index = lax.axis_index(axis)
    if count == 2:
        return paired(array, swapped(array, axis), index == 0, dimension)
    shape = array.shape[:dimension] + (count,) + array.shape[dimension:]
    whole = jnp.zeros(shape, array.dtype)
    for step in range(count):
        piece = array if step == 0 else shifted(array, axis, step)
        whole = lax.dynamic_update_index_in_dim(
            whole, piece, (index + count - step) % count, dimension
        )
    return whole


def sum_rows(partial):
    count = lax.axis_size("to")
    index = lax.axis_index("to")
    width = partial.shape[-1]
    current = partial
    distance = 1
    while distance < count:
        low = (index // distance) % 2
        left = count // (2 * distance)
        shard = partial.shape[0] // count
        view = current.reshape(left, 2, shard, width)
        sent = pick(view, 1 - low, 1).astype(BF16)
        current = pick(view, low, 1) + swapped(sent, "to", distance).astype(F32)
        distance *= 2
    return current.reshape(-1, width)


def gather_rows(shard):
    count = lax.axis_size("to")
    index = lax.axis_index("to")
    rows, width = shard.shape
    current = shard.reshape(1, rows, width)
    distance = count // 2
    while distance >= 1:
        low = (index // distance) % 2
        current = paired(current, swapped(current, "to", distance), low == 0, 1)
        current = current.reshape(-1, rows, width)
        distance //= 2
    return current.reshape(-1, width)


def sum_all(vector):
    for axis in BLOCKS + TENSORS:
        distance = 1
        while distance < lax.axis_size(axis):
            vector = vector + swapped(vector, axis, distance)
            distance *= 2
    return vector


def over_pair(array):
    return jnp.concatenate([array, swapped(array, "ti")], axis=-1)


def over_blocks(array):
    return gather_axis(array, "bo")


def over_cores(array):
    whole = gather_axis(array, "bi", 1)
    return whole.reshape(-1, whole.shape[-1])


def gather_blocks(array):
    count = lax.axis_size("bo")
    mine = jnp.stack([array] + [shifted(array, "bo", step) for step in range(1, count)])
    return jnp.concatenate([mine, swapped(mine, "bi")])


def scatter_blocks(array):
    count = lax.axis_size("bo")
    mine = array[:count] + swapped(array[count:].astype(BF16), "bi").astype(F32)
    low = mine.astype(BF16)
    total = mine[0]
    for step in range(1, count):
        total += shifted(low[step], "bo", count - step).astype(F32)
    return total


def local(
    hidden_in,
    out_grad,
    norm_in,
    w_query,
    key_weight,
    value_weight,
    w_out,
    query_gain,
    key_gain,
    norm_mid,
    w_gate,
    w_up,
    w_down,
):
    block_outers = lax.axis_size("bo")
    blocks = block_outers * lax.axis_size("bi")
    block_outer = lax.axis_index("bo")
    block_inner = lax.axis_index("bi")
    block = block_outer * lax.axis_size("bi") + block_inner
    outer = lax.axis_index("to")
    inner = lax.axis_index("ti")
    pair = lax.axis_size("ti")
    batch, rows, width = hidden_in.shape
    head_dim = query_gain.shape[0] * blocks
    query_width = w_query.shape[1]
    key_width = key_weight.shape[1]
    hidden_units = w_gate.shape[1]
    query_heads = query_width * pair // head_dim
    pair_heads = key_width * pair // head_dim
    group_size = query_heads // pair_heads
    shard_rows = rows // lax.axis_size("to")
    scale = head_dim ** (-0.5)

    own_gains = jnp.concatenate([norm_in, norm_mid, query_gain, key_gain])[None]
    all_gains = gather_axis(gather_axis(own_gains, "bo"), "bi", 1)
    all_gains = all_gains.reshape(blocks, -1).astype(F32)
    part = norm_in.shape[0]
    gain_in = all_gains[:, :part].reshape(-1)
    gain_mid = all_gains[:, part : 2 * part].reshape(-1)
    head_part = query_gain.shape[0]
    gain_query = all_gains[:, 2 * part : 2 * part + head_part].reshape(-1)
    gain_key = all_gains[:, 2 * part + head_part :].reshape(-1)

    query_half = over_pair(w_query)
    kv_half = over_blocks(jnp.concatenate([key_weight, value_weight], axis=1))
    query_most = over_blocks(query_half)
    kv_most = over_pair(kv_half)
    query_full = over_cores(query_most)
    kv_full = over_cores(kv_most)
    out_half = over_pair(after(w_out.T, query_most, kv_most))
    up_half = over_blocks(after(w_up, query_most, kv_most))
    gate_half = over_pair(after(w_gate, out_half))
    out_full = over_cores(over_blocks(out_half))
    down_half = over_blocks(after(w_down.T, up_half))
    gate_full = over_cores(over_blocks(gate_half))
    up_full = over_cores(over_pair(up_half))
    down_full = over_cores(over_pair(down_half))

    positions = block * rows + jnp.arange(rows, dtype=jnp.int32)
    cosine, sine = rotation_tables(positions, head_dim)
    key_blocks = []
    for side in range(2):
        side_inner = block_inner if side == 0 else 1 - block_inner
        for step in range(block_outers):
            owner = (block_outer + block_outers - step) % block_outers
            key_blocks.append(owner * 2 + side_inner)
    key_positions = (
        jnp.stack(key_blocks).astype(jnp.int32)[:, None] * rows
        + jnp.arange(rows, dtype=jnp.int32)[None, :]
    ).reshape(-1)
    visible = key_positions[None, :] <= positions[:, None]

    def prepare(raw, gain):
        return rotate(normed(raw, gain), cosine, sine)

    groups = batch // pair
    own_hidden = pick(hidden_in.reshape(pair, groups, rows, width), inner)
    own_grad = pick(out_grad.reshape(pair, groups, rows, width), inner)
    layer_parts = []
    hidden_parts = []
    kept = []
    vector_terms = 0.0
    for group in range(groups):
        normal_in = normed(own_hidden[group].astype(F32), gain_in).astype(BF16)
        query_raw = dot(normal_in, query_full).reshape(rows, query_heads, head_dim)
        kv_raw = dot(normal_in, kv_full).reshape(rows, pair, 2, -1, head_dim)
        key_raw = kv_raw[:, :, 0].reshape(rows, pair_heads, head_dim)
        value_rows = kv_raw[:, :, 1].reshape(rows, pair_heads, head_dim).astype(BF16)
        query_rows = prepare(query_raw, gain_query).astype(BF16)
        key_rows = prepare(key_raw, gain_key).astype(BF16)
        key_value = gather_blocks(
            jnp.stack([key_rows.transpose(1, 0, 2), value_rows.transpose(1, 0, 2)])
        )
        key_value = key_value.transpose(1, 2, 0, 3, 4).reshape(
            2, pair_heads, blocks * rows, head_dim
        )
        keys, values = key_value[0], key_value[1]
        query_group = query_rows.reshape(rows, pair_heads, group_size, head_dim).transpose(
            1, 2, 0, 3
        )
        scores = jnp.einsum("hgqd,hkd->hgqk", query_group, keys, preferred_element_type=F32) * scale
        scores = jnp.where(visible, scores, -jnp.inf)
        row_max = jnp.max(scores, axis=-1)
        weights = jnp.exp(scores - row_max[..., None])
        row_sum = jnp.sum(weights, axis=-1)
        weighted = jnp.einsum(
            "hgqk,hkd->hgqd", weights.astype(BF16), values, preferred_element_type=F32
        )
        attn_group = weighted / row_sum[..., None]
        log_total = row_max + jnp.log(row_sum)
        attended = attn_group.transpose(2, 0, 1, 3).reshape(rows, -1).astype(BF16)

        start = outer * shard_rows
        x_shard = lax.dynamic_slice_in_dim(own_hidden[group], start, shard_rows, 0).astype(F32)
        grad_out_shard = lax.dynamic_slice_in_dim(own_grad[group], start, shard_rows, 0).astype(F32)
        residual = x_shard + sum_rows(dot_back(attended, out_full))
        mid = gather_rows(normed(residual, gain_mid).astype(BF16))

        grad_active = dot(own_grad[group], down_full)
        gate = dot(mid, gate_full)
        up = dot(mid, up_full)
        slope = jax.nn.sigmoid(gate)
        silu = gate * slope
        active = (silu * up).astype(BF16)
        grad_gate = (grad_active * up * slope * (1.0 + gate * (1.0 - slope))).astype(BF16)
        grad_up = (grad_active * silu).astype(BF16)
        grad_normal_mid = sum_rows(dot_back(grad_gate, gate_full) + dot_back(grad_up, up_full))

        mlp_part = dot_back(active, down_full)

        _, pull_mid = jax.vjp(normed, residual, gain_mid)
        grad_resid_norm, term_gain_mid = pull_mid(grad_normal_mid)
        grad_residual = grad_out_shard + grad_resid_norm
        branch = gather_rows(grad_residual.astype(BF16))
        layer_shard = (residual + sum_rows(after(mlp_part, branch))).astype(BF16)
        grad_attended = dot(branch, out_full).astype(BF16)

        grad_group = grad_attended.reshape(rows, pair_heads, group_size, head_dim).transpose(
            1, 2, 0, 3
        )
        row_dots = jnp.sum(grad_group.astype(F32) * attn_group, axis=-1)
        scores = jnp.einsum("hgqd,hkd->hgqk", query_group, keys, preferred_element_type=F32) * scale
        scores = jnp.where(visible, scores, -jnp.inf)
        probs = jnp.exp(scores - log_total[..., None])
        value_sum = jnp.einsum(
            "hgqk,hgqd->hkd", probs.astype(BF16), grad_group, preferred_element_type=F32
        )
        grad_probs = jnp.einsum("hgqd,hkd->hgqk", grad_group, values, preferred_element_type=F32)
        grad_scores = (probs * (grad_probs - row_dots[..., None]) * scale).astype(BF16)
        grad_query = jnp.einsum("hgqk,hkd->hgqd", grad_scores, keys, preferred_element_type=F32)
        key_sum = jnp.einsum(
            "hgqk,hgqd->hkd", grad_scores, query_group, preferred_element_type=F32
        )
        sums = jnp.stack([key_sum, value_sum]).reshape(2, pair_heads, blocks, rows, head_dim)
        shares = scatter_blocks(sums.transpose(2, 0, 1, 3, 4))
        grad_query = grad_query.transpose(2, 0, 1, 3).reshape(rows, query_heads, head_dim)
        _, pull_query = jax.vjp(prepare, query_raw, gain_query)
        grad_query_raw, term_query_gain = pull_query(grad_query)
        _, pull_key = jax.vjp(prepare, key_raw, gain_key)
        grad_key_raw, term_key_gain = pull_key(shares[0].transpose(1, 0, 2))
        grad_query_low = grad_query_raw.reshape(rows, -1).astype(BF16)
        grad_kv_low = (
            jnp.stack(
                [
                    grad_key_raw.reshape(rows, pair, -1),
                    shares[1].transpose(1, 0, 2).reshape(rows, pair, -1),
                ],
                axis=2,
            )
            .reshape(rows, -1)
            .astype(BF16)
        )
        grad_normal_in = sum_rows(
            after(
                dot_back(grad_query_low, query_full) + dot_back(grad_kv_low, kv_full), layer_shard
            )
        )
        _, pull_first = jax.vjp(normed, x_shard, gain_in)
        grad_x_norm, term_gain_in = pull_first(grad_normal_in)
        hidden_shard = (grad_residual + grad_x_norm).astype(BF16)
        layer_rows = gather_rows(layer_shard)
        layer_parts.append(gather_axis(layer_rows, "ti"))
        hidden_parts.append(gather_axis(gather_rows(after(hidden_shard, layer_rows)), "ti"))

        vector_terms += jnp.concatenate(
            [term_gain_in, term_gain_mid, term_query_gain, term_key_gain]
        )
        kept.append(
            (normal_in, grad_query_low, grad_kv_low, attended, branch, mid, grad_gate, grad_up, active)
        )

    normal_in, grad_query_low, grad_kv_low, attended, branch, mid, grad_gate, grad_up, active = (
        jnp.concatenate(parts) for parts in zip(*kept)
    )

    def in_order(array):
        own, other = jnp.split(array, 2, axis=1)
        return paired(own, other, inner == 0, 0)

    def weight_sum(left, right):
        term = jnp.concatenate(
            [
                jnp.einsum("td,tc->dc", left, right[i], preferred_element_type=F32).astype(BF16)
                for i in range(pair)
            ]
        )
        return lax.psum_scatter(
            term, ("ti", "bo", "bi"), scatter_dimension=0, tiled=True
        ).astype(F32)

    share_gu = weight_sum(mid, jnp.concatenate([in_order(grad_gate), in_order(grad_up)], axis=-1))
    grad_down = weight_sum(own_grad.reshape(-1, width), in_order(active)).T
    grad_out_w = weight_sum(branch, in_order(attended)).T
    share_qkv = weight_sum(
        normal_in, jnp.concatenate([in_order(grad_query_low), in_order(grad_kv_low)], axis=-1)
    )

    vectors = sum_all(vector_terms[None])[0]

    def vector_share(first, size):
        return lax.dynamic_slice_in_dim(vectors, first + block * (size // blocks), size // blocks)

    def whole_batch(parts):
        return jnp.stack(parts, axis=1).reshape(batch, rows, width)

    return (
        whole_batch(layer_parts),
        whole_batch(hidden_parts),
        vector_share(0, width),
        share_qkv[:, :query_width],
        share_qkv[:, query_width : query_width + key_width],
        share_qkv[:, query_width + key_width :],
        grad_out_w,
        vector_share(2 * width, head_dim),
        vector_share(2 * width + head_dim, head_dim),
        vector_share(width, width),
        share_gu[:, :hidden_units],
        share_gu[:, hidden_units:],
        grad_down,
    )


def solution(mesh):
    block_count, tensor_count = mesh.devices.shape
    split = Mesh(
        mesh.devices.reshape(block_count // 2, 2, tensor_count // 2, 2), BLOCKS + TENSORS
    )
    row_weight = P(BLOCKS, TENSORS)
    column_weight = P(TENSORS, BLOCKS)
    tokens = P(None, BLOCKS, None)
    vector = P(BLOCKS)
    weights = (
        vector,
        row_weight,
        row_weight,
        row_weight,
        column_weight,
        vector,
        vector,
        vector,
        row_weight,
        row_weight,
        column_weight,
    )
    return jax.shard_map(
        local,
        mesh=split,
        in_specs=(tokens, tokens) + weights,
        out_specs=(tokens, tokens) + weights,
        check_vma=False,
    )
```

```python
import functools

import jax
import jax.numpy as jnp
from jax import lax
from jax.experimental import pallas as pl
from jax.experimental.pallas import tpu as pltpu
from jax.sharding import Mesh
from jax.sharding import PartitionSpec as P

EPSILON = 1e-06
ROTARY_BASE = 1000000.0
BF16 = jnp.bfloat16
F32 = jnp.float32
BLOCKS = ("bo", "bi")
TENSORS = ("to", "ti")
HIDDEN_CHUNK = 512
VMEM_LIMIT = 48 * 1024 * 1024


def normed(values, gain):
    return values * lax.rsqrt(jnp.mean(values * values, axis=-1, keepdims=True) + EPSILON) * gain


def rotation_tables(positions, head_dim):
    half = head_dim // 2
    inverse = jnp.power(F32(ROTARY_BASE), -(jnp.arange(half, dtype=F32) * 2.0 / head_dim))
    angles = positions.astype(F32)[:, None] * inverse[None, :]
    cosine, sine = jnp.cos(angles), jnp.sin(angles)
    return jnp.concatenate([cosine, cosine], -1), jnp.concatenate([-sine, sine], -1)


def after(array, *earlier):
    return lax.optimization_barrier((array,) + earlier)[0]


def shifted(array, axis, step):
    count = lax.axis_size(axis)
    return lax.ppermute(array, axis, [(i, (i + step) % count) for i in range(count)])


def swapped(array, axis, distance=1):
    count = lax.axis_size(axis)
    return lax.ppermute(array, axis, [(i, i ^ distance) for i in range(count)])


def pick(array, index, dimension=0):
    return lax.dynamic_index_in_dim(array, index, dimension, keepdims=False)


def paired(own, other, first, dimension):
    return jnp.where(
        first, jnp.stack([own, other], dimension), jnp.stack([other, own], dimension)
    )


def gather_axis(array, axis, dimension=0):
    count = lax.axis_size(axis)
    index = lax.axis_index(axis)
    if count == 2:
        return paired(array, swapped(array, axis), index == 0, dimension)
    shape = array.shape[:dimension] + (count,) + array.shape[dimension:]
    whole = jnp.zeros(shape, array.dtype)
    for step in range(count):
        piece = array if step == 0 else shifted(array, axis, step)
        whole = lax.dynamic_update_index_in_dim(
            whole, piece, (index + count - step) % count, dimension
        )
    return whole


def sum_rows(kept, sent):
    count = lax.axis_size("to")
    index = lax.axis_index("to")
    rows, width = kept.shape
    shard = 2 * rows // count
    current = kept + swapped(sent, "to", 1).astype(F32)
    distance = 2
    while distance < count:
        low = (index // distance) % 2
        view = current.reshape(-1, 2, shard, width)
        sent = pick(view, 1 - low, 1).astype(BF16)
        current = pick(view, low, 1) + swapped(sent, "to", distance).astype(F32)
        distance *= 2
    return current.reshape(-1, width)


def gather_rows(shard):
    count = lax.axis_size("to")
    index = lax.axis_index("to")
    rows, width = shard.shape
    current = shard.reshape(1, rows, width)
    distance = count // 2
    while distance >= 1:
        low = (index // distance) % 2
        current = paired(current, swapped(current, "to", distance), low == 0, 1)
        current = current.reshape(-1, rows, width)
        distance //= 2
    return current.reshape(-1, width)


def sum_all(vector):
    for axis in BLOCKS + TENSORS:
        distance = 1
        while distance < lax.axis_size(axis):
            vector = vector + swapped(vector, axis, distance)
            distance *= 2
    return vector


def over_pair(array):
    return jnp.concatenate([array, swapped(array, "ti")], axis=-1)


def over_blocks(array):
    count = lax.axis_size("bo")
    return jnp.stack([array] + [shifted(array, "bo", step) for step in range(1, count)])


def over_cores(array):
    return array, swapped(array, "bi")


def mxu(left, right):
    return jnp.dot(left, right, preferred_element_type=F32)


def mxu_back(left, right):
    return lax.dot_general(left, right, (((1,), (1,)), ((), ())), preferred_element_type=F32)


def mxu_outer(left, right):
    return lax.dot_general(left, right, (((0,), (0,)), ((), ())), preferred_element_type=F32)


def columns(info, position, size):
    return pl.ds(pl.multiple_of(info[1 + position] * size, 128), size)


def project(info, rows_ref, mine, theirs):
    count, size = mine.shape[0], mine.shape[1]
    total = None
    for position in range(2 * count):
        block = mine[position] if position < count else theirs[position - count]
        term = mxu(rows_ref[:, columns(info, position, size)], block)
        total = term if total is None else total + term
    return total


def project_back(info, grads, mine, theirs, position):
    count = mine.shape[0]
    block = mine[position] if position < count else theirs[position - count]
    return mxu_back(grads, block)


def row_block(info, rows, count, position, own):
    shard = rows // count
    low = info[0] if own else 1 - info[0]
    return pl.ds(pl.multiple_of((2 * position + low) * shard, shard), shard)


def unit(values):
    return lax.rsqrt(jnp.mean(values * values, axis=-1, keepdims=True) + EPSILON)


def swap_halves(values):
    return pltpu.roll(values, values.shape[-1] // 2, 1)


def prepare_kernel(
    sizes,
    info,
    x_ref,
    gain_ref,
    query_gain_ref,
    key_gain_ref,
    cosine_ref,
    sine_ref,
    query_mine,
    query_theirs,
    kv_mine,
    kv_theirs,
    normal_ref,
    query_raw_ref,
    key_raw_ref,
    query_ref,
    kv_ref,
):
    head_dim, pair_heads, key_heads = sizes
    x = x_ref[...].astype(F32)
    normal_ref[...] = (x * unit(x) * gain_ref[...]).astype(BF16)
    cosine, sine = cosine_ref[...], sine_ref[...]

    def rotated(raw, gain):
        values = raw * unit(raw) * gain
        return (values * cosine + swap_halves(values) * sine).astype(BF16)

    query_raw = project(info, normal_ref, query_mine, query_theirs)
    query_raw_ref[...] = query_raw
    for head in range(query_raw.shape[1] // head_dim):
        part = slice(head * head_dim, (head + 1) * head_dim)
        query_ref[:, part] = rotated(query_raw[:, part], query_gain_ref[...])
    kv_raw = project(info, normal_ref, kv_mine, kv_theirs)
    for head in range(pair_heads):
        start = (2 * key_heads * (head // key_heads) + head % key_heads) * head_dim
        raw = kv_raw[:, start : start + head_dim]
        key_raw_ref[:, head * head_dim : (head + 1) * head_dim] = raw
        kv_ref[0, head] = rotated(raw, key_gain_ref[...])
        start += key_heads * head_dim
        kv_ref[1, head] = kv_raw[:, start : start + head_dim].astype(BF16)


def visible_scores(info, queries, keys, position, blocks, rows, scale):
    scores = mxu_back(queries, keys) * scale
    if position == 0:
        query_rows = lax.broadcasted_iota(jnp.int32, scores.shape, 0) % rows
        key_rows = lax.broadcasted_iota(jnp.int32, scores.shape, 1)
        return jnp.where(key_rows <= query_rows, scores, -jnp.inf)
    return jnp.where(info[1 + blocks + position] > 0, scores, -jnp.inf)


def attend_kernel(
    sizes,
    info,
    query_ref,
    kv_mine,
    kv_theirs,
    out_mine,
    out_theirs,
    attn_ref,
    log_ref,
    attended_ref,
    kept_ref,
    sent_ref,
    scores_ref,
):
    head_dim, pair_heads, group, counts = sizes
    rows = query_ref.shape[0]
    half = kv_mine.shape[0]
    scale = head_dim ** (-0.5)
    lanes = lax.broadcasted_iota(jnp.int32, (rows, head_dim), 1)
    logs = jnp.zeros((rows, head_dim), F32)

    def key_value(which, position, head):
        ref = kv_mine if position < half else kv_theirs
        return ref[position % half, which, head]

    for head in range(pair_heads):
        queries = jnp.concatenate(
            [
                query_ref[:, (head * group + i) * head_dim : (head * group + i + 1) * head_dim]
                for i in range(group)
            ]
        )
        top = None
        for position in range(2 * half):
            scores = visible_scores(
                info, queries, key_value(0, position, head), position, 2 * half, rows, scale
            )
            scores_ref[position] = scores
            block_top = jnp.max(scores, axis=-1, keepdims=True)
            top = block_top if top is None else jnp.maximum(top, block_top)
        total = jnp.zeros_like(top)
        weighted = jnp.zeros((group * rows, head_dim), F32)
        for position in range(2 * half):
            weights = jnp.exp(scores_ref[position] - top)
            total += jnp.sum(weights, axis=-1, keepdims=True)
            weighted += mxu(weights.astype(BF16), key_value(1, position, head))
        attn = weighted / total
        log_total = top + jnp.log(total)
        for i in range(group):
            index = head * group + i
            part = slice(index * head_dim, (index + 1) * head_dim)
            piece = attn[i * rows : (i + 1) * rows]
            attn_ref[:, part] = piece
            attended_ref[:, part] = piece.astype(BF16)
            logs = jnp.where(lanes == index, log_total[i * rows : (i + 1) * rows], logs)
    log_ref[...] = logs
    for own, target in ((True, kept_ref), (False, sent_ref)):
        chosen = jnp.concatenate(
            [
                attended_ref[row_block(info, rows, counts, j, own), :]
                for j in range(counts // 2)
            ]
        )
        for position in range(2 * half):
            target[:, columns(info, position, out_mine.shape[1])] = project_back(
                info, chosen, out_mine, out_theirs, position
            ).astype(target.dtype)


def feed_forward_kernel(
    counts,
    info,
    mid_ref,
    grad_ref,
    gate_mine,
    gate_theirs,
    up_mine,
    up_theirs,
    down_mine,
    down_theirs,
    active_ref,
    grad_gate_ref,
    grad_up_ref,
    grad_kept,
    grad_sent,
    mlp_kept,
    mlp_sent,
    grad_total,
    mlp_total,
):
    step = pl.program_id(0)
    rows = mid_ref.shape[0]
    half, size = gate_mine.shape[0], gate_mine.shape[1]
    gate = project(info, mid_ref, gate_mine, gate_theirs)
    up = project(info, mid_ref, up_mine, up_theirs)
    grad = project(info, grad_ref, down_mine, down_theirs)
    slope = jax.nn.sigmoid(gate)
    silu = gate * slope
    active = (silu * up).astype(BF16)
    grad_gate = (grad * up * slope * (1.0 + gate * (1.0 - slope))).astype(BF16)
    grad_up = (grad * silu).astype(BF16)
    active_ref[...] = active
    grad_gate_ref[...] = grad_gate
    grad_up_ref[...] = grad_up

    def term(position):
        part = columns(info, position, size)
        grad_term = project_back(
            info, grad_gate, gate_mine, gate_theirs, position
        ) + project_back(info, grad_up, up_mine, up_theirs, position)
        return part, grad_term, project_back(info, active, down_mine, down_theirs, position)

    @pl.when(step == 0)
    def _():
        for position in range(2 * half):
            part, grad_term, mlp_term = term(position)
            grad_total[:, part] = grad_term
            mlp_total[:, part] = mlp_term

    @pl.when(step > 0)
    def _():
        for position in range(2 * half):
            part, grad_term, mlp_term = term(position)
            grad_total[:, part] += grad_term
            mlp_total[:, part] += mlp_term

    @pl.when(step == pl.num_programs(0) - 1)
    def _():
        shard = rows // counts
        for j in range(counts // 2):
            place = slice(j * shard, (j + 1) * shard)
            for own, grad_out, mlp_out in (
                (True, grad_kept, mlp_kept),
                (False, grad_sent, mlp_sent),
            ):
                source = row_block(info, rows, counts, j, own)
                grad_out[place, :] = grad_total[source, :].astype(grad_out.dtype)
                mlp_out[place, :] = mlp_total[source, :].astype(mlp_out.dtype)


def attend_back_kernel(
    sizes,
    info,
    branch_ref,
    out_mine,
    out_theirs,
    query_ref,
    kv_mine,
    kv_theirs,
    attn_ref,
    log_ref,
    grad_query_ref,
    kept_ref,
    sent_ref,
):
    head_dim, pair_heads, group = sizes
    rows = query_ref.shape[0]
    half = kv_mine.shape[0]
    scale = head_dim ** (-0.5)
    grad_attended = project(info, branch_ref, out_mine, out_theirs).astype(BF16)

    def key_value(which, position, head):
        ref = kv_mine if position < half else kv_theirs
        return ref[position % half, which, head]

    for head in range(pair_heads):
        parts = [
            slice((head * group + i) * head_dim, (head * group + i + 1) * head_dim)
            for i in range(group)
        ]
        queries = jnp.concatenate([query_ref[:, part] for part in parts])
        grads = jnp.concatenate([grad_attended[:, part] for part in parts])
        attn = jnp.concatenate([attn_ref[:, part] for part in parts])
        logs = jnp.concatenate(
            [log_ref[:, head * group + i : head * group + i + 1] for i in range(group)]
        )
        row_dots = jnp.sum(grads.astype(F32) * attn, axis=-1, keepdims=True)
        grad_query = jnp.zeros((group * rows, head_dim), F32)
        for position in range(2 * half):
            keys = key_value(0, position, head)
            scores = visible_scores(info, queries, keys, position, 2 * half, rows, scale)
            probs = jnp.exp(scores - logs)
            grad_probs = mxu_back(grads, key_value(1, position, head))
            grad_scores = (probs * (grad_probs - row_dots) * scale).astype(BF16)
            grad_query += mxu(grad_scores, keys)
            target = kept_ref if position < half else sent_ref
            target[position % half, 0, head] = mxu_outer(grad_scores, queries).astype(target.dtype)
            target[position % half, 1, head] = mxu_outer(probs.astype(BF16), grads).astype(
                target.dtype
            )
        for i, part in enumerate(parts):
            grad_query_ref[:, part] = grad_query[i * rows : (i + 1) * rows]


def finish_kernel(
    sizes,
    info,
    grad_query_ref,
    query_raw_ref,
    key_raw_ref,
    shares_ref,
    query_gain_ref,
    key_gain_ref,
    cosine_ref,
    sine_ref,
    query_mine,
    query_theirs,
    kv_mine,
    kv_theirs,
    query_low_ref,
    kv_low_ref,
    gains_ref,
    kept_ref,
    sent_ref,
):
    head_dim, pair_heads, key_heads, counts = sizes
    rows = grad_query_ref.shape[0]
    cosine, sine = cosine_ref[...], sine_ref[...]

    def back(grad, raw, gain):
        grad = grad * cosine - swap_halves(grad) * sine
        scale = unit(raw)
        gain_term = jnp.sum(grad * raw * scale, axis=0, keepdims=True)
        inner = grad * gain
        mean = jnp.mean(inner * raw, axis=-1, keepdims=True)
        return (scale * inner - raw * (scale * scale * scale * mean)).astype(BF16), gain_term

    total = jnp.zeros((1, head_dim), F32)
    for head in range(query_raw_ref.shape[1] // head_dim):
        part = slice(head * head_dim, (head + 1) * head_dim)
        query_low_ref[:, part], term = back(
            grad_query_ref[:, part], query_raw_ref[:, part], query_gain_ref[...]
        )
        total += term
    gains_ref[0:1, :] = total
    total = jnp.zeros((1, head_dim), F32)
    for head in range(pair_heads):
        start = (2 * key_heads * (head // key_heads) + head % key_heads) * head_dim
        kv_low_ref[:, start : start + head_dim], term = back(
            shares_ref[0, head],
            key_raw_ref[:, head * head_dim : (head + 1) * head_dim],
            key_gain_ref[...],
        )
        total += term
        start += key_heads * head_dim
        kv_low_ref[:, start : start + head_dim] = shares_ref[1, head].astype(BF16)
    gains_ref[1:2, :] = total
    for own, target in ((True, kept_ref), (False, sent_ref)):
        places = [row_block(info, rows, counts, j, own) for j in range(counts // 2)]
        query_low = jnp.concatenate([query_low_ref[place, :] for place in places])
        kv_low = jnp.concatenate([kv_low_ref[place, :] for place in places])
        for position in range(2 * query_mine.shape[0]):
            target[:, columns(info, position, query_mine.shape[1])] = (
                project_back(info, query_low, query_mine, query_theirs, position)
                + project_back(info, kv_low, kv_mine, kv_theirs, position)
            ).astype(target.dtype)


def weight_kernel(groups, products, info, *refs):
    inputs, out_ref = refs[:-1], refs[-1]
    place = 0
    for index, (left, rights) in enumerate(products):
        lefts = [inputs[left * groups + g][...] for g in range(groups)]
        for right in rights:
            total = None
            for g in range(groups):
                term = mxu_outer(lefts[g], inputs[right * groups + g][...])
                total = term if total is None else total + term
            size = total.shape[1]
            if out_ref.ndim == 5:
                out_ref[0, 0, place] = total.astype(BF16)
                place += 1
            else:
                out_ref[0, 0, :, place : place + size] = total.astype(BF16)
                place += size


def call(kernel, operands, outputs, scratch=(), flops=0, memory=()):
    smem = pl.BlockSpec(memory_space=pltpu.SMEM)
    vmem = pl.BlockSpec(memory_space=pltpu.VMEM)
    moved = sum(a.size * a.dtype.itemsize for a in tuple(operands[1:]) + tuple(outputs))
    return pl.pallas_call(
        kernel,
        out_shape=tuple(outputs),
        in_specs=[smem] + [vmem] * (len(operands) - 1),
        out_specs=tuple(vmem for _ in outputs),
        scratch_shapes=list(scratch),
        compiler_params=pltpu.CompilerParams(vmem_limit_bytes=VMEM_LIMIT),
        cost_estimate=pl.CostEstimate(flops=flops, bytes_accessed=moved, transcendentals=0),
    )(*operands)


def shape(dims, dtype):
    return jax.ShapeDtypeStruct(dims, dtype)


def weight_blocks(info, lefts, rights, products, blocks, pair, stacked):
    groups = len(lefts[0])
    rows, width = lefts[0][0].shape
    size = width // blocks
    operands, specs = [], []
    for members in lefts:
        for array in members:
            operands.append(array)
            specs.append(pl.BlockSpec((rows, size), lambda t, b, info: (0, b)))
    for members in rights:
        for array in members:
            operands.append(array)
            specs.append(
                pl.BlockSpec(
                    (rows, array.shape[1] // pair),
                    lambda t, b, info: (0, lax.rem(t + info[0], 2)),
                )
            )
    widths = [array.shape[1] // pair for array, *_ in rights]
    if stacked:
        dims = (pair, blocks, len(rights), size, widths[0])
        out_spec = pl.BlockSpec((1, 1) + dims[2:], lambda t, b, info: (t, b, 0, 0, 0))
    else:
        dims = (pair, blocks, size, sum(widths))
        out_spec = pl.BlockSpec((1, 1) + dims[2:], lambda t, b, info: (t, b, 0, 0))
    shifted_products = [
        (left, [len(lefts) + right for right in columns_of]) for left, columns_of in products
    ]
    flops = 2 * groups * rows * width * pair * sum(widths)
    moved = 2 * pair * width * sum(widths)
    return pl.pallas_call(
        functools.partial(weight_kernel, groups, shifted_products),
        out_shape=shape(dims, BF16),
        grid_spec=pltpu.PrefetchScalarGridSpec(
            num_scalar_prefetch=1,
            grid=(pair, blocks),
            in_specs=specs,
            out_specs=out_spec,
        ),
        compiler_params=pltpu.CompilerParams(vmem_limit_bytes=VMEM_LIMIT),
        cost_estimate=pl.CostEstimate(flops=flops, bytes_accessed=moved, transcendentals=0),
    )(info, *operands)


def local(
    hidden_in,
    out_grad,
    norm_in,
    w_query,
    key_weight,
    value_weight,
    w_out,
    query_gain,
    key_gain,
    norm_mid,
    w_gate,
    w_up,
    w_down,
):
    block_outers = lax.axis_size("bo")
    blocks = block_outers * lax.axis_size("bi")
    block_outer = lax.axis_index("bo")
    block_inner = lax.axis_index("bi")
    block = block_outer * lax.axis_size("bi") + block_inner
    outer = lax.axis_index("to")
    inner = lax.axis_index("ti")
    pair = lax.axis_size("ti")
    counts = lax.axis_size("to")
    batch, rows, width = hidden_in.shape
    head_dim = query_gain.shape[0] * blocks
    query_width = w_query.shape[1]
    key_width = key_weight.shape[1]
    hidden_units = w_gate.shape[1]
    key_heads = key_width // head_dim
    query_heads = query_width * pair // head_dim
    pair_heads = key_heads * pair
    group_size = query_heads // pair_heads
    shard_rows = rows // counts

    own_gains = jnp.concatenate([norm_in, norm_mid, query_gain, key_gain])[None]
    all_gains = gather_axis(gather_axis(own_gains, "bo"), "bi", 1)
    all_gains = all_gains.reshape(blocks, -1).astype(F32)
    part = norm_in.shape[0]
    gain_in = all_gains[:, :part].reshape(-1)
    gain_mid = all_gains[:, part : 2 * part].reshape(-1)
    head_part = query_gain.shape[0]
    gain_query = all_gains[:, 2 * part : 2 * part + head_part].reshape(1, -1)
    gain_key = all_gains[:, 2 * part + head_part :].reshape(1, -1)

    query_half = over_pair(w_query)
    kv_half = over_blocks(jnp.concatenate([key_weight, value_weight], axis=1))
    query_most = over_blocks(query_half)
    kv_most = over_pair(kv_half)
    query_full = over_cores(query_most)
    kv_full = over_cores(kv_most)
    out_half = over_pair(after(w_out.T, query_most, kv_most))
    up_half = over_blocks(after(w_up, query_most, kv_most))
    gate_half = over_pair(after(w_gate, out_half))
    out_full = over_cores(over_blocks(out_half))
    down_half = over_blocks(after(w_down.T, up_half))
    gate_full = over_cores(over_blocks(gate_half))
    up_full = over_cores(over_pair(up_half))
    down_full = over_cores(over_pair(down_half))

    positions = block * rows + jnp.arange(rows, dtype=jnp.int32)
    cosine, sine = rotation_tables(positions, head_dim)
    block_ids = []
    for side in range(2):
        side_inner = block_inner if side == 0 else 1 - block_inner
        for step in range(block_outers):
            owner = lax.rem(block_outer + block_outers - step, block_outers)
            block_ids.append(owner * 2 + side_inner)
    info = jnp.stack(
        [lax.rem(outer, 2)] + block_ids + [(b < block).astype(jnp.int32) for b in block_ids]
    ).astype(jnp.int32)
    inner_info = inner.astype(jnp.int32)[None]

    groups = batch // pair
    own_hidden = pick(hidden_in.reshape(pair, groups, rows, width), inner)
    own_grad = pick(out_grad.reshape(pair, groups, rows, width), inner)
    half_rows = rows // 2
    halves = (shape((half_rows, width), F32), shape((half_rows, width), BF16))
    all_heads = query_heads * head_dim
    all_keys = pair_heads * head_dim
    kv_dims = (2, pair_heads, rows, head_dim)
    layer_parts = []
    hidden_parts = []
    kept = []
    vector_terms = 0.0
    for group in range(groups):
        normal_in, query_raw, key_raw, query_rows, kv_rows = call(
            functools.partial(prepare_kernel, (head_dim, pair_heads, key_heads)),
            (info, own_hidden[group], gain_in[None], gain_query, gain_key, cosine, sine)
            + query_full
            + kv_full,
            (
                shape((rows, width), BF16),
                shape((rows, all_heads), F32),
                shape((rows, all_keys), F32),
                shape((rows, all_heads), BF16),
                shape(kv_dims, BF16),
            ),
            flops=2 * rows * width * (all_heads + 2 * all_keys),
        )
        key_value = over_cores(over_blocks(kv_rows))
        attn, log_total, attended, out_kept, out_sent = call(
            functools.partial(attend_kernel, (head_dim, pair_heads, group_size, counts)),
            (info, query_rows) + key_value + out_full,
            (
                shape((rows, all_heads), F32),
                shape((rows, head_dim), F32),
                shape((rows, all_heads), BF16),
            )
            + halves,
            scratch=[pltpu.VMEM((blocks, group_size * rows, rows), F32)],
            flops=2 * rows * all_heads * (width + 4 * blocks * rows),
        )

        start = outer * shard_rows
        x_shard = lax.dynamic_slice_in_dim(own_hidden[group], start, shard_rows, 0).astype(F32)
        grad_out_shard = lax.dynamic_slice_in_dim(own_grad[group], start, shard_rows, 0).astype(F32)
        residual = x_shard + sum_rows(out_kept, out_sent)
        mid = gather_rows(normed(residual, gain_mid).astype(BF16))

        whole = pl.BlockSpec((rows, width), lambda i: (0, 0))
        weight = pl.BlockSpec(
            (block_outers, width // blocks, HIDDEN_CHUNK), lambda i: (0, 0, i)
        )
        piece = pl.BlockSpec((rows, HIDDEN_CHUNK), lambda i: (0, i))
        half_spec = pl.BlockSpec((half_rows, width), lambda i: (0, 0))
        hidden_shape = shape((rows, pair * hidden_units), BF16)
        active, grad_gate, grad_up, grad_kept, grad_sent, mlp_kept, mlp_sent = pl.pallas_call(
            functools.partial(feed_forward_kernel, counts),
            out_shape=(hidden_shape,) * 3 + halves + halves,
            grid=(pair * hidden_units // HIDDEN_CHUNK,),
            in_specs=[pl.BlockSpec(memory_space=pltpu.SMEM), whole, whole] + [weight] * 6,
            out_specs=(piece,) * 3 + (half_spec,) * 4,
            scratch_shapes=[pltpu.VMEM((rows, width), F32)] * 2,
            compiler_params=pltpu.CompilerParams(vmem_limit_bytes=VMEM_LIMIT),
            cost_estimate=pl.CostEstimate(
                flops=12 * rows * width * pair * hidden_units,
                bytes_accessed=6 * width * pair * hidden_units,
                transcendentals=rows * pair * hidden_units,
            ),
        )(info, mid, own_grad[group], *gate_full, *up_full, *down_full)
        grad_normal_mid = sum_rows(grad_kept, grad_sent)

        _, pull_mid = jax.vjp(normed, residual, gain_mid)
        grad_resid_norm, term_gain_mid = pull_mid(grad_normal_mid)
        grad_residual = grad_out_shard + grad_resid_norm
        branch = gather_rows(grad_residual.astype(BF16))
        layer_shard = (residual + sum_rows(mlp_kept, after(mlp_sent, branch))).astype(BF16)

        side_dims = (block_outers,) + kv_dims
        grad_query, kv_kept, kv_sent = call(
            functools.partial(attend_back_kernel, (head_dim, pair_heads, group_size)),
            (info, branch) + out_full + (query_rows,) + key_value + (attn, log_total),
            (shape((rows, all_heads), F32), shape(side_dims, F32), shape(side_dims, BF16)),
            flops=2 * rows * all_heads * (width + 10 * blocks * rows),
        )
        mine = kv_kept + swapped(kv_sent, "bi").astype(F32)
        low = mine.astype(BF16)
        shares = mine[0]
        for step in range(1, block_outers):
            shares += shifted(low[step], "bo", block_outers - step).astype(F32)
        grad_query_low, grad_kv_low, gain_terms, in_kept, in_sent = call(
            functools.partial(finish_kernel, (head_dim, pair_heads, key_heads, counts)),
            (info, grad_query, query_raw, key_raw, shares, gain_query, gain_key, cosine, sine)
            + query_full
            + kv_full,
            (
                shape((rows, all_heads), BF16),
                shape((rows, 2 * all_keys), BF16),
                shape((2, head_dim), F32),
            )
            + halves,
            flops=2 * rows * width * (all_heads + 2 * all_keys),
        )
        grad_normal_in = sum_rows(in_kept, after(in_sent, layer_shard))
        _, pull_first = jax.vjp(normed, x_shard, gain_in)
        grad_x_norm, term_gain_in = pull_first(grad_normal_in)
        hidden_shard = (grad_residual + grad_x_norm).astype(BF16)
        layer_rows = gather_rows(layer_shard)
        layer_parts.append(gather_axis(layer_rows, "ti"))
        hidden_parts.append(gather_axis(gather_rows(after(hidden_shard, layer_rows)), "ti"))

        vector_terms += jnp.concatenate([term_gain_in, term_gain_mid, gain_terms.reshape(-1)])
        kept.append(
            (normal_in, grad_query_low, grad_kv_low, attended, branch, mid)
            + (own_grad[group], grad_gate, grad_up, active)
        )

    (
        normal_in,
        grad_query_low,
        grad_kv_low,
        attended,
        branch,
        mid,
        grad_rows,
        grad_gate,
        grad_up,
        active,
    ) = zip(*kept)

    def weight_sum(terms):
        flat = terms.reshape((-1,) + terms.shape[-1:])
        share = lax.psum_scatter(flat, ("ti", "bo", "bi"), scatter_dimension=0, tiled=True)
        return share.astype(F32).reshape(terms.shape[2:])

    share_mlp = weight_sum(
        weight_blocks(
            inner_info,
            (mid, grad_rows),
            (grad_gate, grad_up, active),
            [(0, [0, 1]), (1, [2])],
            blocks,
            pair,
            True,
        )
    )
    share_attn = weight_sum(
        weight_blocks(
            inner_info,
            (normal_in, branch),
            (grad_query_low, grad_kv_low, attended),
            [(0, [0, 1]), (1, [2])],
            blocks,
            pair,
            False,
        )
    )
    vectors = sum_all(vector_terms[None])[0]

    def vector_share(first, size):
        return lax.dynamic_slice_in_dim(vectors, first + block * (size // blocks), size // blocks)

    def whole_batch(parts):
        return jnp.stack(parts, axis=1).reshape(batch, rows, width)

    kv_start = query_width + 2 * key_width
    return (
        whole_batch(layer_parts),
        whole_batch(hidden_parts),
        vector_share(0, width),
        share_attn[:, :query_width],
        share_attn[:, query_width : query_width + key_width],
        share_attn[:, query_width + key_width : kv_start],
        share_attn[:, kv_start:].T,
        vector_share(2 * width, head_dim),
        vector_share(2 * width + head_dim, head_dim),
        vector_share(width, width),
        share_mlp[0],
        share_mlp[1],
        share_mlp[2].T,
    )


def solution(mesh):
    block_count, tensor_count = mesh.devices.shape
    split = Mesh(
        mesh.devices.reshape(block_count // 2, 2, tensor_count // 2, 2), BLOCKS + TENSORS
    )
    row_weight = P(BLOCKS, TENSORS)
    column_weight = P(TENSORS, BLOCKS)
    tokens = P(None, BLOCKS, None)
    vector = P(BLOCKS)
    weights = (
        vector,
        row_weight,
        row_weight,
        row_weight,
        column_weight,
        vector,
        vector,
        vector,
        row_weight,
        row_weight,
        column_weight,
    )
    return jax.shard_map(
        local,
        mesh=split,
        in_specs=(tokens, tokens) + weights,
        out_specs=(tokens, tokens) + weights,
        check_vma=False,
    )
```

```python
import functools

import jax
import jax.numpy as jnp
from jax import lax
from jax.experimental import pallas as pl
from jax.experimental.layout import Layout, with_layout_constraint
from jax.experimental.pallas import tpu as pltpu
from jax.sharding import Mesh
from jax.sharding import PartitionSpec as P

EPSILON = 1e-06
ROTARY_BASE = 1000000.0
BF16 = jnp.bfloat16
F32 = jnp.float32
BLOCKS = ("bo", "bi")
TENSORS = ("to", "ti")
HIDDEN_CHUNK = 768
VMEM_LIMIT = 48 * 1024 * 1024


def normed(values, gain):
    return values * lax.rsqrt(jnp.mean(values * values, axis=-1, keepdims=True) + EPSILON) * gain


def rotation_tables(positions, head_dim):
    half = head_dim // 2
    inverse = jnp.power(F32(ROTARY_BASE), -(jnp.arange(half, dtype=F32) * 2.0 / head_dim))
    angles = positions.astype(F32)[:, None] * inverse[None, :]
    cosine, sine = jnp.cos(angles), jnp.sin(angles)
    return jnp.concatenate([cosine, cosine], -1), jnp.concatenate([-sine, sine], -1)


def after(array, *earlier):
    if not earlier:
        return array
    return lax.optimization_barrier((array,) + earlier)[0]


def together(arrays, earlier):
    arrays = tuple(arrays)
    if not earlier:
        return arrays
    return tuple(lax.optimization_barrier(arrays + tuple(earlier))[: len(arrays)])


def shifted(array, axis, step):
    count = lax.axis_size(axis)
    return lax.ppermute(array, axis, [(i, (i + step) % count) for i in range(count)])


def swapped(array, axis, distance=1):
    count = lax.axis_size(axis)
    return lax.ppermute(array, axis, [(i, i ^ distance) for i in range(count)])


def pick(array, index, dimension=0):
    return lax.dynamic_index_in_dim(array, index, dimension, keepdims=False)


def paired(own, other, first, dimension):
    return jnp.where(
        first, jnp.stack([own, other], dimension), jnp.stack([other, own], dimension)
    )


def gather_axis(array, axis, dimension=0):
    count = lax.axis_size(axis)
    index = lax.axis_index(axis)
    if count == 2:
        return paired(array, swapped(array, axis), index == 0, dimension)
    shape = array.shape[:dimension] + (count,) + array.shape[dimension:]
    whole = jnp.zeros(shape, array.dtype)
    for step in range(count):
        piece = array if step == 0 else shifted(array, axis, step)
        whole = lax.dynamic_update_index_in_dim(
            whole, piece, (index + count - step) % count, dimension
        )
    return whole


class Chain:
    def __init__(self):
        self.done = []

    def swap(self, arrays, distances, before=(), during=()):
        before = tuple(a for some in before for a in some) + (self.done[-2] if len(self.done) > 1 else ())
        arrays = together(arrays, before)
        arrived = tuple(swapped(a, "to", d) for a, d in zip(arrays, distances))
        arrived = together(arrived, during)
        self.done.append(arrived)
        return arrived


def sum_rows(chain, first_kept, first_sent, second_kept, second_sent, before=(), during=()):
    count = lax.axis_size("to")
    index = lax.axis_index("to")
    rows, width = first_kept.shape
    shard = 2 * rows // count
    near, far = 1, count // 2
    while True:
        arrived = chain.swap((first_sent, second_sent), (near, far), before[:1], during)
        before, during = before[1:], ()
        first = first_kept + arrived[0].astype(F32)
        second = second_kept + arrived[1].astype(F32)
        near, far = 2 * near, far // 2
        yield
        if far < 1:
            return jnp.concatenate([first, second], axis=-1)
        bit = lax.rem(index // near, 2)
        view = first.reshape(-1, 2, shard, width)
        first_sent = pick(view, 1 - bit, 1).astype(BF16).reshape(-1, width)
        first_kept = pick(view, bit, 1).reshape(-1, width)
        bit = lax.rem(index // far, 2)
        view = second.reshape(2, -1, width)
        second_sent = pick(view, 1 - bit).astype(BF16)
        second_kept = pick(view, bit)


def gather_rows(chain, shard, before=()):
    before = tuple(before)
    count = lax.axis_size("to")
    index = lax.axis_index("to")
    rows = shard.shape[0]
    width = shard.shape[1] // 2
    first, second = shard[None, :, :width], shard[None, :, width:]
    far, near = count // 2, 1
    while far >= 1:
        arrived = chain.swap((first, second), (far, near), before[:1])
        before = before[1:]
        first = paired(first, arrived[0], lax.rem(index // far, 2) == 0, 1)
        second = paired(second, arrived[1], lax.rem(index // near, 2) == 0, 0)
        first = first.reshape(-1, rows, width)
        second = second.reshape(-1, rows, width)
        far, near = far // 2, 2 * near
        yield
    return jnp.concatenate([first.reshape(-1, width), second.reshape(-1, width)], axis=-1)


def gather_parts(chain, shard, before=()):
    rows = shard.shape[0]
    width = shard.shape[1] // 2
    first, second = shard[None, :, :width], shard[None, :, width:]
    far, near = lax.axis_size("to") // 2, 1
    while True:
        arrived = chain.swap((first, second), (far, near), before[:1])
        before = before[1:]
        far, near = far // 2, 2 * near
        yield
        if far < 1:
            return first, arrived[0], second, arrived[1]
        first = jnp.concatenate([first, arrived[0]])
        second = jnp.concatenate([second, arrived[1]])


def gather_masks(count):
    orders = []
    for distances in (lambda i: count >> (i + 1), lambda i: 1 << i):
        masks = [0]
        for i in range(count.bit_length() - 1):
            masks += [mask | distances(i) for mask in masks]
        orders.append(masks)
    return orders


def run(*stages):
    results = [None] * len(stages)
    left = dict(enumerate(stages))
    while left:
        for index in list(left):
            try:
                next(left[index])
            except StopIteration as end:
                results[index] = end.value
                del left[index]
    return results


def sum_over(vector, axes):
    for axis in axes:
        distance = 1
        while distance < lax.axis_size(axis):
            vector = vector + swapped(vector, axis, distance)
            distance *= 2
    return vector


def over_pair(array, late=()):
    return jnp.concatenate([array, after(swapped(array, "ti"), *late)], axis=-1)


def over_blocks(array, late=()):
    count = lax.axis_size("bo")
    arrived = [after(shifted(array, "bo", step), *late) for step in range(1, count)]
    return jnp.stack([array] + arrived)


def over_cores(array):
    return array, swapped(array, "bi")


LOW, HIGH, INNER, FIRST, OUTER, PLACES = 0, 1, 2, 3, 4, 5


def mxu(left, right):
    return jnp.dot(left, right, preferred_element_type=F32)


def mxu_back(left, right):
    return lax.dot_general(left, right, (((1,), (1,)), ((), ())), preferred_element_type=F32)


def mxu_outer(left, right):
    return lax.dot_general(left, right, (((0,), (0,)), ((), ())), preferred_element_type=F32)


def columns(info, position, size):
    if info is None:
        return slice(position * size, (position + 1) * size)
    return pl.ds(pl.multiple_of(info[PLACES + position] * size, 128), size)


def project(info, rows_ref, *weights):
    blocks = [(ref, i) for ref in weights for i in range(ref.shape[0])]
    total = None
    for position, (ref, i) in enumerate(blocks):
        term = mxu(rows_ref[:, columns(info, position, ref.shape[1])], ref[i])
        total = term if total is None else total + term
    return total


def project_back(grads, position, *weights):
    blocks = [(ref, i) for ref in weights for i in range(ref.shape[0])]
    ref, i = blocks[position]
    return mxu_back(grads, ref[i])


def write_halves(info, counts, total_ref, outputs):
    first_kept, first_sent, second_kept, second_sent = outputs
    rows, width = total_ref.shape
    shard, middle = rows // counts, width // 2
    for j in range(counts // 2):
        for target, bit in ((first_kept, info[LOW]), (first_sent, 1 - info[LOW])):
            source = pl.ds(pl.multiple_of((2 * j + bit) * shard, shard), shard)
            target[j, 0] = total_ref[source, :middle].astype(target.dtype)
        for target, bit in ((second_kept, info[HIGH]), (second_sent, 1 - info[HIGH])):
            source = pl.ds(pl.multiple_of((bit * (counts // 2) + j) * shard, shard), shard)
            target[j, 0] = total_ref[source, middle:].astype(target.dtype)


def read_parts(info, counts, parts, target):
    rows, width = target.shape
    shard, middle = rows // counts, width // 2
    for side, masks in enumerate(gather_masks(counts)):
        for i, mask in enumerate(masks):
            ref = parts[2 * side + 2 * i // counts]
            place = pl.multiple_of(jnp.bitwise_xor(info[OUTER], mask) * shard, shard)
            columns_now = slice(side * middle, (side + 1) * middle)
            target[pl.ds(place, shard), columns_now] = ref[i % (counts // 2), 0]


def unit(values):
    return lax.rsqrt(jnp.mean(values * values, axis=-1, keepdims=True) + EPSILON)


def swap_halves(values):
    return pltpu.roll(values, values.shape[-1] // 2, 1)


def prepare_kernel(
    sizes,
    info,
    x_ref,
    gain_ref,
    query_gain_ref,
    key_gain_ref,
    cosine_ref,
    sine_ref,
    query_mine,
    query_theirs,
    kv_mine,
    kv_theirs,
    normal_ref,
    query_raw_ref,
    key_raw_ref,
    query_ref,
    kv_ref,
):
    head_dim, pair_heads, key_heads = sizes
    x = x_ref[0].astype(F32)
    normal_ref, query_raw_ref, key_raw_ref, query_ref, kv_ref = (
        ref.at[0] for ref in (normal_ref, query_raw_ref, key_raw_ref, query_ref, kv_ref)
    )
    normal_ref[...] = (x * unit(x) * gain_ref[...]).astype(BF16)
    cosine, sine = cosine_ref[...], sine_ref[...]

    def rotated(raw, gain):
        values = raw * unit(raw) * gain
        return (values * cosine + swap_halves(values) * sine).astype(BF16)

    query_raw = project(info, normal_ref, query_mine, query_theirs)
    query_raw_ref[...] = query_raw
    for head in range(query_raw.shape[1] // head_dim):
        part = slice(head * head_dim, (head + 1) * head_dim)
        query_ref[:, part] = rotated(query_raw[:, part], query_gain_ref[...])
    kv_raw = project(info, normal_ref, kv_mine, kv_theirs)
    for head in range(pair_heads):
        start = (2 * key_heads * (head // key_heads) + head % key_heads) * head_dim
        raw = kv_raw[:, start : start + head_dim]
        key_raw_ref[:, head * head_dim : (head + 1) * head_dim] = raw
        kv_ref[0, head] = rotated(raw, key_gain_ref[...])
        start += key_heads * head_dim
        kv_ref[1, head] = kv_raw[:, start : start + head_dim].astype(BF16)


def visible_scores(info, queries, keys, position, blocks, rows, scale):
    scores = mxu_back(queries, keys) * scale
    if position == 0:
        query_rows = lax.broadcasted_iota(jnp.int32, scores.shape, 0) % rows
        key_rows = lax.broadcasted_iota(jnp.int32, scores.shape, 1)
        return jnp.where(key_rows <= query_rows, scores, -jnp.inf)
    return jnp.where(info[PLACES + blocks + position] > 0, scores, -jnp.inf)


def attend_kernel(
    sizes,
    info,
    query_ref,
    kv_mine,
    kv_theirs,
    out_mine,
    out_theirs,
    attn_ref,
    log_ref,
    attended_ref,
    first_kept,
    first_sent,
    second_kept,
    second_sent,
    scores_ref,
    total_ref,
):
    head_dim, pair_heads, group, counts = sizes
    query_ref, attn_ref, log_ref, attended_ref = (
        ref.at[0] for ref in (query_ref, attn_ref, log_ref, attended_ref)
    )
    rows = query_ref.shape[0]
    half = kv_mine.shape[0]
    scale = head_dim ** (-0.5)
    lanes = lax.broadcasted_iota(jnp.int32, (rows, head_dim), 1)
    logs = jnp.zeros((rows, head_dim), F32)

    def key_value(which, position, head):
        ref = kv_mine if position < half else kv_theirs
        return ref[position % half, 0, which, head]

    for head in range(pair_heads):
        queries = jnp.concatenate(
            [
                query_ref[:, (head * group + i) * head_dim : (head * group + i + 1) * head_dim]
                for i in range(group)
            ]
        )
        top = None
        for position in range(2 * half):
            scores = visible_scores(
                info, queries, key_value(0, position, head), position, 2 * half, rows, scale
            )
            scores_ref[position] = scores
            block_top = jnp.max(scores, axis=-1, keepdims=True)
            top = block_top if top is None else jnp.maximum(top, block_top)
        total = jnp.zeros_like(top)
        weighted = jnp.zeros((group * rows, head_dim), F32)
        for position in range(2 * half):
            weights = jnp.exp(scores_ref[position] - top)
            total += jnp.sum(weights, axis=-1, keepdims=True)
            weighted += mxu(weights.astype(BF16), key_value(1, position, head))
        attn = weighted / total
        log_total = top + jnp.log(total)
        for i in range(group):
            index = head * group + i
            part = slice(index * head_dim, (index + 1) * head_dim)
            piece = attn[i * rows : (i + 1) * rows]
            attn_ref[:, part] = piece
            attended_ref[:, part] = piece.astype(BF16)
            logs = jnp.where(lanes == index, log_total[i * rows : (i + 1) * rows], logs)
    log_ref[...] = logs
    attended = attended_ref[...]
    for position in range(2 * half):
        total_ref[:, columns(info, position, out_mine.shape[1])] = project_back(
            attended, position, out_mine, out_theirs
        )
    write_halves(info, counts, total_ref, (first_kept, first_sent, second_kept, second_sent))


def feed_forward_kernel(
    counts,
    info,
    first_own,
    first_other,
    second_own,
    second_other,
    grad_ref,
    gate_ref,
    up_ref,
    down_ref,
    active_ref,
    grad_gate_ref,
    grad_up_ref,
    mid_ref,
    *outputs,
):
    grad_total, mlp_total = outputs[8:]
    step = pl.program_id(0)

    @pl.when(step == 0)
    def _():
        read_parts(info, counts, (first_own, first_other, second_own, second_other), mid_ref)

    blocks, size = gate_ref.shape[0], gate_ref.shape[1]
    gate = project(None, mid_ref, gate_ref)
    up = project(None, mid_ref, up_ref)
    grad = project(None, grad_ref.at[0], down_ref)
    slope = jax.nn.sigmoid(gate)
    silu = gate * slope
    active = (silu * up).astype(BF16)
    grad_gate = (grad * up * slope * (1.0 + gate * (1.0 - slope))).astype(BF16)
    grad_up = (grad * silu).astype(BF16)
    active_ref[...] = active
    grad_gate_ref[...] = grad_gate
    grad_up_ref[...] = grad_up

    def term(position):
        part = columns(None, position, size)
        grad_term = project_back(grad_gate, position, gate_ref) + project_back(
            grad_up, position, up_ref
        )
        return part, grad_term, project_back(active, position, down_ref)

    @pl.when(step == 0)
    def _():
        for position in range(blocks):
            part, grad_term, mlp_term = term(position)
            grad_total[:, part] = grad_term
            mlp_total[:, part] = mlp_term

    @pl.when(step > 0)
    def _():
        for position in range(blocks):
            part, grad_term, mlp_term = term(position)
            grad_total[:, part] += grad_term
            mlp_total[:, part] += mlp_term

    @pl.when(step == pl.num_programs(0) - 1)
    def _():
        write_halves(info, counts, grad_total, outputs[:4])
        write_halves(info, counts, mlp_total, outputs[4:8])


def attend_back_kernel(
    sizes,
    info,
    first_own,
    first_other,
    second_own,
    second_other,
    out_mine,
    out_theirs,
    query_ref,
    kv_mine,
    kv_theirs,
    attn_ref,
    log_ref,
    branch_ref,
    grad_query_ref,
    kept_ref,
    sent_ref,
):
    head_dim, pair_heads, group, counts = sizes
    query_ref, attn_ref, log_ref, branch_ref, grad_query_ref = (
        ref.at[0] for ref in (query_ref, attn_ref, log_ref, branch_ref, grad_query_ref)
    )
    read_parts(info, counts, (first_own, first_other, second_own, second_other), branch_ref)
    rows = query_ref.shape[0]
    half = kv_mine.shape[0]
    scale = head_dim ** (-0.5)
    grad_attended = project(info, branch_ref, out_mine, out_theirs).astype(BF16)

    def key_value(which, position, head):
        ref = kv_mine if position < half else kv_theirs
        return ref[position % half, 0, which, head]

    for head in range(pair_heads):
        parts = [
            slice((head * group + i) * head_dim, (head * group + i + 1) * head_dim)
            for i in range(group)
        ]
        queries = jnp.concatenate([query_ref[:, part] for part in parts])
        grads = jnp.concatenate([grad_attended[:, part] for part in parts])
        attn = jnp.concatenate([attn_ref[:, part] for part in parts])
        logs = jnp.concatenate(
            [log_ref[:, head * group + i : head * group + i + 1] for i in range(group)]
        )
        row_dots = jnp.sum(grads.astype(F32) * attn, axis=-1, keepdims=True)
        grad_query = jnp.zeros((group * rows, head_dim), F32)
        for position in range(2 * half):
            keys = key_value(0, position, head)
            scores = visible_scores(info, queries, keys, position, 2 * half, rows, scale)
            probs = jnp.exp(scores - logs)
            grad_probs = mxu_back(grads, key_value(1, position, head))
            grad_scores = (probs * (grad_probs - row_dots) * scale).astype(BF16)
            grad_query += mxu(grad_scores, keys)
            target = kept_ref if position < half else sent_ref
            target[position % half, 0, 0, head] = mxu_outer(grad_scores, queries).astype(target.dtype)
            target[position % half, 0, 1, head] = mxu_outer(probs.astype(BF16), grads).astype(
                target.dtype
            )
        for i, part in enumerate(parts):
            grad_query_ref[:, part] = grad_query[i * rows : (i + 1) * rows]


def finish_kernel(
    sizes,
    info,
    grad_query_ref,
    query_raw_ref,
    key_raw_ref,
    shares_ref,
    query_gain_ref,
    key_gain_ref,
    cosine_ref,
    sine_ref,
    query_mine,
    query_theirs,
    kv_mine,
    kv_theirs,
    query_low_ref,
    kv_low_ref,
    gains_ref,
    first_kept,
    first_sent,
    second_kept,
    second_sent,
    total_ref,
):
    head_dim, pair_heads, key_heads, counts = sizes
    grad_query_ref, query_raw_ref, key_raw_ref, shares_ref, query_low_ref, kv_low_ref, gains_ref = (
        ref.at[0]
        for ref in (
            grad_query_ref,
            query_raw_ref,
            key_raw_ref,
            shares_ref,
            query_low_ref,
            kv_low_ref,
            gains_ref,
        )
    )
    cosine, sine = cosine_ref[...], sine_ref[...]

    def back(grad, raw, gain):
        grad = grad * cosine - swap_halves(grad) * sine
        scale = unit(raw)
        gain_term = jnp.sum(grad * raw * scale, axis=0, keepdims=True)
        inner = grad * gain
        mean = jnp.mean(inner * raw, axis=-1, keepdims=True)
        return (scale * inner - raw * (scale * scale * scale * mean)).astype(BF16), gain_term

    total = jnp.zeros((1, head_dim), F32)
    for head in range(query_raw_ref.shape[1] // head_dim):
        part = slice(head * head_dim, (head + 1) * head_dim)
        query_low_ref[:, part], term = back(
            grad_query_ref[:, part], query_raw_ref[:, part], query_gain_ref[...]
        )
        total += term
    gains_ref[0:1, :] = total
    total = jnp.zeros((1, head_dim), F32)
    for head in range(pair_heads):
        start = (2 * key_heads * (head // key_heads) + head % key_heads) * head_dim
        kv_low_ref[:, start : start + head_dim], term = back(
            shares_ref[0, head],
            key_raw_ref[:, head * head_dim : (head + 1) * head_dim],
            key_gain_ref[...],
        )
        total += term
        start += key_heads * head_dim
        kv_low_ref[:, start : start + head_dim] = shares_ref[1, head].astype(BF16)
    gains_ref[1:2, :] = total
    query_low, kv_low = query_low_ref[...], kv_low_ref[...]
    for position in range(2 * query_mine.shape[0]):
        total_ref[:, columns(info, position, query_mine.shape[1])] = project_back(
            query_low, position, query_mine, query_theirs
        ) + project_back(kv_low, position, kv_mine, kv_theirs)
    write_halves(info, counts, total_ref, (first_kept, first_sent, second_kept, second_sent))


def weight_kernel(counts, products, info, *refs):
    arrays, start = [], 0
    for count in counts:
        arrays.append(refs[start : start + count])
        start += count
    out_ref = refs[-1]

    def rows_of(members):
        flat = [ref[...].reshape(-1, ref.shape[-1]) for ref in members]
        return flat[0] if len(flat) == 1 else jnp.concatenate(flat)

    place = 0
    for left, rights in products:
        left_rows = rows_of(arrays[left])
        for right in rights:
            total = mxu_outer(left_rows, rows_of(arrays[right])).astype(BF16)
            if len(out_ref.shape) == 5:
                out_ref[0, 0, place] = total
                place += 1
            else:
                out_ref[0, 0, :, place : place + total.shape[1]] = total
                place += total.shape[1]


def whole_spec(dims):
    return pl.BlockSpec(dims, lambda i, info: (0,) * len(dims))


def group_spec(array, dimension=0):
    dims = array.shape[:dimension] + (1,) + array.shape[dimension + 1 :]
    rest = len(dims) - dimension - 1
    return pl.BlockSpec(dims, lambda g, info: (0,) * dimension + (g,) + (0,) * rest)


def group_call(kernel, groups, info, operands, outputs, scratch=(), flops=0):
    moved = sum(a.size * a.dtype.itemsize for a, _ in tuple(operands) + tuple(outputs))
    return pl.pallas_call(
        kernel,
        out_shape=[a for a, _ in outputs],
        grid_spec=pltpu.PrefetchScalarGridSpec(
            num_scalar_prefetch=1,
            grid=(groups,),
            in_specs=[spec for _, spec in operands],
            out_specs=[spec for _, spec in outputs],
            scratch_shapes=list(scratch),
        ),
        compiler_params=pltpu.CompilerParams(vmem_limit_bytes=VMEM_LIMIT),
        cost_estimate=pl.CostEstimate(flops=flops, bytes_accessed=moved, transcendentals=0),
    )(info, *[a for a, _ in operands])


def shape(dims, dtype):
    return jax.ShapeDtypeStruct(dims, dtype)


def weight_blocks(info, lefts, rights, products, blocks, pair, stacked, in_order):
    width = lefts[0][0].shape[-1]
    size = width // blocks
    batch_rows = sum(a.shape[0] for a in lefts[0]) if lefts[0][0].ndim == 2 else None
    operands, specs = [], []
    for array in [a for members in lefts for a in members]:
        operands.append(array)
        if array.ndim == 2:
            spec = pl.BlockSpec((array.shape[0], size), lambda t, b, info: (0, b))
        elif array.shape[0] * array.shape[1] == batch_rows or batch_rows is None:
            spec = pl.BlockSpec(array.shape[:2] + (size,), lambda t, b, info: (0, 0, b))
        else:
            spec = pl.BlockSpec(
                (array.shape[0] // pair, array.shape[1], size),
                lambda t, b, info: (info[INNER], 0, b),
            )
        specs.append(spec)
    widths = []
    for members in rights:
        widths.append(members[0].shape[-1] // pair)
        for array in members:
            operands.append(array)
            dims = array.shape[:-1] + (array.shape[-1] // pair,)
            zeros = (0,) * (array.ndim - 1)
            specs.append(
                pl.BlockSpec(
                    dims,
                    lambda t, b, info, zeros=zeros: zeros
                    + (t if in_order else lax.rem(t + info[INNER], 2),),
                )
            )
    if stacked:
        dims = (pair, blocks, len(rights), size, widths[0])
        out_spec = pl.BlockSpec((1, 1) + dims[2:], lambda t, b, info: (t, b, 0, 0, 0))
    else:
        dims = (pair, blocks, size, sum(widths))
        out_spec = pl.BlockSpec((1, 1) + dims[2:], lambda t, b, info: (t, b, 0, 0))
    counts = [len(members) for members in tuple(lefts) + tuple(rights)]
    placed = [(left, [len(lefts) + right for right in columns_of]) for left, columns_of in products]
    rows = rights[0][0].size * len(rights[0]) // rights[0][0].shape[-1]
    flops = 2 * rows * width * pair * sum(widths)
    moved = 2 * pair * width * sum(widths)
    return pl.pallas_call(
        functools.partial(weight_kernel, counts, placed),
        out_shape=shape(dims, BF16),
        grid_spec=pltpu.PrefetchScalarGridSpec(
            num_scalar_prefetch=1,
            grid=(pair, blocks),
            in_specs=specs,
            out_specs=out_spec,
        ),
        compiler_params=pltpu.CompilerParams(vmem_limit_bytes=VMEM_LIMIT),
        cost_estimate=pl.CostEstimate(flops=flops, bytes_accessed=moved, transcendentals=0),
    )(info, *operands)


def local(
    hidden_in,
    out_grad,
    norm_in,
    w_query,
    key_weight,
    value_weight,
    w_out,
    query_gain,
    key_gain,
    norm_mid,
    w_gate,
    w_up,
    w_down,
):
    block_outers = lax.axis_size("bo")
    blocks = block_outers * lax.axis_size("bi")
    block_outer = lax.axis_index("bo")
    block_inner = lax.axis_index("bi")
    block = block_outer * lax.axis_size("bi") + block_inner
    outer = lax.axis_index("to")
    inner = lax.axis_index("ti")
    pair = lax.axis_size("ti")
    counts = lax.axis_size("to")
    batch, rows, width = hidden_in.shape
    head_dim = query_gain.shape[0] * blocks
    query_width = w_query.shape[1]
    key_width = key_weight.shape[1]
    hidden_units = w_gate.shape[1]
    key_heads = key_width // head_dim
    query_heads = query_width * pair // head_dim
    pair_heads = key_heads * pair
    group_size = query_heads // pair_heads
    shard_rows = rows // counts

    query_half = over_pair(w_query)
    kv_half = over_blocks(jnp.concatenate([key_weight, value_weight], axis=1))
    query_most = over_blocks(query_half)
    kv_most = over_pair(kv_half)
    query_full = over_cores(query_most)
    kv_full = over_cores(kv_most)
    out_half = over_blocks(after(w_out.T, query_half))
    mlp_own = jnp.concatenate([w_gate, w_up, w_down.T], axis=1)
    mlp_own = with_layout_constraint(after(mlp_own, query_most, kv_most), Layout((0, 1)))
    mlp_weights = lax.all_gather(mlp_own, ("ti", "bo", "bi"), axis=0)

    own_gains = jnp.concatenate([norm_in, norm_mid, query_gain, key_gain])[None]
    own_gains = after(own_gains, kv_half)
    all_gains = gather_axis(gather_axis(own_gains, "bo"), "bi", 1)
    all_gains = all_gains.reshape(blocks, -1).astype(F32)
    part = norm_in.shape[0]
    gain_in = all_gains[:, :part].reshape(-1)
    gain_mid = all_gains[:, part : 2 * part].reshape(-1)
    head_part = query_gain.shape[0]
    gain_query = all_gains[:, 2 * part : 2 * part + head_part].reshape(1, -1)
    gain_key = all_gains[:, 2 * part + head_part :].reshape(1, -1)

    positions = block * rows + jnp.arange(rows, dtype=jnp.int32)
    cosine, sine = rotation_tables(positions, head_dim)
    block_ids = []
    for side in range(2):
        side_inner = block_inner if side == 0 else 1 - block_inner
        for step in range(block_outers):
            owner = lax.rem(block_outer + block_outers - step, block_outers)
            block_ids.append(owner * 2 + side_inner)
    groups = batch // pair
    first_sequence = inner * groups
    info = jnp.stack(
        [lax.rem(outer, 2), outer // (counts // 2), inner, first_sequence, outer]
        + block_ids
        + [(b < block).astype(jnp.int32) for b in block_ids]
    ).astype(jnp.int32)

    chain = Chain()
    all_heads = query_heads * head_dim
    all_keys = pair_heads * head_dim
    kv_dims = (groups, 2, pair_heads, rows, head_dim)
    side_dims = (block_outers,) + kv_dims
    half_dims = (counts // 2, groups, shard_rows, width // 2)
    whole_rows = pltpu.VMEM((rows, width), F32)

    def by_group(dims, dtype, dimension=0):
        array = shape(dims, dtype)
        return array, group_spec(array, dimension)

    def per_group(*arrays):
        return tuple((a, group_spec(a)) for a in arrays)

    def per_second(*arrays):
        return tuple((a, group_spec(a, 1)) for a in arrays)

    def shared(*arrays):
        return tuple((a, whole_spec(a.shape)) for a in arrays)

    halves = (by_group(half_dims, F32, 1), by_group(half_dims, BF16, 1)) * 2

    def flat(parts):
        return [part.reshape(-1, part.shape[-1]) for part in parts]

    def own_sequences(array):
        return (array, pl.BlockSpec((1, rows, width), lambda g, info: (info[FIRST] + g, 0, 0)))

    normal_in, query_raw, key_raw, query_rows, kv_rows = group_call(
        functools.partial(prepare_kernel, (head_dim, pair_heads, key_heads)),
        groups,
        info,
        (own_sequences(hidden_in),)
        + shared(after(gain_in[None], out_half), gain_query, gain_key, cosine, sine)
        + shared(*query_full, *kv_full),
        (
            by_group((groups, rows, width), BF16),
            by_group((groups, rows, all_heads), F32),
            by_group((groups, rows, all_keys), F32),
            by_group((groups, rows, all_heads), BF16),
            by_group(kv_dims, BF16),
        ),
        flops=2 * groups * rows * width * (all_heads + 2 * all_keys),
    )
    kv_blocks = over_blocks(kv_rows)
    key_value = over_cores(kv_blocks)
    out_full = over_cores(over_pair(out_half, (kv_blocks,)))
    attn, log_total, attended, *out_parts = group_call(
        functools.partial(attend_kernel, (head_dim, pair_heads, group_size, counts)),
        groups,
        info,
        per_group(query_rows) + per_second(*key_value) + shared(*out_full),
        (
            by_group((groups, rows, all_heads), F32),
            by_group((groups, rows, head_dim), F32),
            by_group((groups, rows, all_heads), BF16),
        )
        + halves,
        scratch=[pltpu.VMEM((blocks, group_size * rows, rows), F32), whole_rows],
        flops=2 * groups * rows * all_heads * (width + 4 * blocks * rows),
    )

    def own_shard(array):
        starts = (first_sequence, outer * shard_rows, 0)
        part = lax.dynamic_slice(array, starts, (groups, shard_rows, width))
        return part.reshape(-1, width).astype(F32)

    x_shard = own_shard(hidden_in)
    grad_out_shard = own_shard(out_grad)
    residual = x_shard + run(sum_rows(chain, *flat(out_parts)))[0]
    normal_mid = normed(residual, gain_mid).astype(BF16).reshape(groups, shard_rows, width)
    mid_parts = []
    for group in range(groups):
        mid_parts += run(gather_parts(chain, normal_mid[group]))

    chunks = pair * hidden_units // HIDDEN_CHUNK
    steps = hidden_units // HIDDEN_CHUNK
    weight_dims = (blocks, width // blocks, HIDDEN_CHUNK)

    def weight_spec(place):
        return pl.BlockSpec(
            weight_dims, lambda i, info: (i // steps, 0, place * steps + lax.rem(i, steps))
        )

    piece = pl.BlockSpec((rows, HIDDEN_CHUNK), lambda i, info: (0, i))
    hidden_shape = shape((rows, pair * hidden_units), BF16)
    one_dims = (counts // 2, 1, shard_rows, width // 2)
    one_halves = (shape(one_dims, F32), shape(one_dims, BF16)) * 4
    mid, active, grad_gate, grad_up, grad_parts, mlp_parts = [], [], [], [], [], []
    for group in range(groups):
        parts = [part.reshape(one_dims) for part in mid_parts[group]]
        sequence = pl.BlockSpec(
            (1, rows, width), lambda i, info, group=group: (info[FIRST] + group, 0, 0)
        )
        results = pl.pallas_call(
            functools.partial(feed_forward_kernel, counts),
            out_shape=(hidden_shape,) * 3 + (shape((rows, width), BF16),) + one_halves,
            grid_spec=pltpu.PrefetchScalarGridSpec(
                num_scalar_prefetch=1,
                grid=(chunks,),
                in_specs=[whole_spec(one_dims)] * 4 + [sequence] + [weight_spec(i) for i in range(3)],
                out_specs=(piece,) * 3 + (whole_spec((rows, width)),) + (whole_spec(one_dims),) * 8,
                scratch_shapes=[whole_rows] * 2,
            ),
            compiler_params=pltpu.CompilerParams(vmem_limit_bytes=VMEM_LIMIT),
            cost_estimate=pl.CostEstimate(
                flops=12 * rows * width * pair * hidden_units,
                bytes_accessed=6 * width * pair * hidden_units,
                transcendentals=rows * pair * hidden_units,
            ),
        )(info, *parts, out_grad, mlp_weights, mlp_weights, mlp_weights)
        active.append(results[0])
        grad_gate.append(results[1])
        grad_up.append(results[2])
        mid.append(results[3])
        grad_parts.append(results[4:8])
        mlp_parts.append(results[8:])

    grad_normal_mid, mlp_sums = [], []
    first_arrived = ()
    for group in range(groups - 1):
        stages = [
            sum_rows(chain, *flat(parts[group]), during=(active[-1],))
            for parts in (grad_parts, mlp_parts)
        ]
        mark = len(chain.done)
        grad_sum, mlp_sum = run(*stages)
        first_arrived = chain.done[mark]
        grad_normal_mid.append(grad_sum)
        mlp_sums.append(mlp_sum)
    mlp_terms = weight_blocks(
        after(info, *first_arrived),
        (mid, [out_grad]),
        (grad_gate, grad_up, active),
        [(0, [0, 1]), (1, [2])],
        blocks,
        pair,
        True,
        True,
    )
    grad_normal_mid += run(sum_rows(chain, *flat(grad_parts[-1]), during=(mlp_terms,)))
    _, pull_mid = jax.vjp(normed, residual, gain_mid)
    grad_norm, gain_mid_term = pull_mid(jnp.concatenate(grad_normal_mid))
    grad_residual = grad_out_shard + grad_norm
    (branch_parts,) = run(gather_parts(chain, grad_residual.astype(BF16)))
    branch_first = chain.done[-2][0]
    branch_parts = [part.reshape(half_dims) for part in branch_parts]
    branch, grad_query, kv_kept, kv_sent = group_call(
        functools.partial(attend_back_kernel, (head_dim, pair_heads, group_size, counts)),
        groups,
        info,
        per_second(*branch_parts)
        + shared(*out_full)
        + per_group(query_rows)
        + per_second(*key_value)
        + per_group(attn, log_total),
        (
            by_group((groups, rows, width), BF16),
            by_group((groups, rows, all_heads), F32),
            by_group(side_dims, F32, 1),
            by_group(side_dims, BF16, 1),
        ),
        flops=2 * groups * rows * all_heads * (width + 10 * blocks * rows),
    )

    def layer_rows(group, mlp_sum):
        part = jnp.split(lax.optimization_barrier(residual), groups)[group]
        return (part + mlp_sum).astype(BF16)

    layer_first = [layer_rows(group, mlp_sums[group]) for group in range(groups - 1)]
    stages = [sum_rows(chain, *flat(mlp_parts[-1]), before=((grad_query,),))]
    stages += [gather_rows(chain, shard, ((grad_query,),)) for shard in layer_first]
    mlp_sum, *layer_whole = run(*stages)
    layer_last = layer_rows(groups - 1, mlp_sum)
    layer_both = [gather_axis(whole, "ti") for whole in layer_whole]
    done_before = tuple(a for done in chain.done[-len(stages) :] for a in done)

    mine = kv_kept + swapped(kv_sent, "bi").astype(F32)
    low = mine.astype(BF16)
    shares = mine[0]
    for step in range(1, block_outers):
        shares += shifted(low[step], "bo", block_outers - step).astype(F32)
    grad_query_low, grad_kv_low, gain_terms, *in_parts = group_call(
        functools.partial(finish_kernel, (head_dim, pair_heads, key_heads, counts)),
        groups,
        info,
        per_group(grad_query, query_raw, key_raw, shares)
        + shared(gain_query, gain_key, cosine, sine, *query_full, *kv_full),
        (
            by_group((groups, rows, all_heads), BF16),
            by_group((groups, rows, 2 * all_keys), BF16),
            by_group((groups, 2, head_dim), F32),
        )
        + halves,
        scratch=[whole_rows],
        flops=2 * groups * rows * width * (all_heads + 2 * all_keys),
    )
    attn_terms = weight_blocks(
        info,
        ([normal_in], [branch]),
        ([grad_query_low], [grad_kv_low], [attended]),
        [(0, [0, 1]), (1, [2])],
        blocks,
        pair,
        False,
        False,
    )

    in_parts = flat(in_parts)
    (grad_normal_in,) = run(
        sum_rows(
            chain, *in_parts, before=(done_before, tuple(layer_both)), during=(attn_terms,)
        )
    )
    _, pull_first = jax.vjp(normed, x_shard, gain_in)
    grad_norm, gain_in_term = pull_first(grad_normal_in)
    hidden_shard = (grad_residual + grad_norm).astype(BF16).reshape(groups, shard_rows, width)

    def weight_sum(terms):
        flat = terms.reshape((-1,) + terms.shape[-1:])
        raw = lax.psum_scatter(flat, ("ti", "bo", "bi"), scatter_dimension=0, tiled=True)
        share = with_layout_constraint(raw, Layout((0, 1)))
        return share.astype(F32).reshape(terms.shape[2:]), raw

    share_mlp, mlp_raw = weight_sum(after(mlp_terms, branch_first))
    share_attn, _ = weight_sum(after(attn_terms, mlp_raw))
    vectors = jnp.concatenate([gain_in_term, gain_mid_term, gain_terms.sum(0).reshape(-1)])
    vectors = sum_over(vectors[None], ("ti",))
    hidden_pairs = [
        gather_axis(hidden_shard[group], "ti").reshape(-1, width)
        for group in range(groups // 2, groups)
    ]
    first = (tuple(hidden_pairs) + (vectors,),)
    stages = [gather_rows(chain, layer_last)]
    stages += [gather_rows(chain, hidden_shard[group], first) for group in range(groups // 2)]
    layer_whole, *hidden_whole = run(*stages)
    layer_both.append(gather_axis(layer_whole, "ti"))
    hidden_both = [gather_axis(whole, "ti") for whole in hidden_whole]
    for both in hidden_pairs:
        (whole,) = run(gather_rows(chain, both))
        whole = whole.reshape(counts, pair, shard_rows, width)
        hidden_both.append(whole.transpose(1, 0, 2, 3).reshape(pair, rows, width))
    vectors = sum_over(vectors, BLOCKS + ("to",))[0]

    def vector_share(first, size):
        return lax.dynamic_slice_in_dim(vectors, first + block * (size // blocks), size // blocks)

    kv_start = query_width + 2 * key_width
    return (
        jnp.stack(layer_both, axis=1).reshape(batch, rows, width),
        jnp.stack(hidden_both, axis=1).reshape(batch, rows, width),
        vector_share(0, width),
        share_attn[:, :query_width],
        share_attn[:, query_width : query_width + key_width],
        share_attn[:, query_width + key_width : kv_start],
        share_attn[:, kv_start:].T,
        vector_share(2 * width, head_dim),
        vector_share(2 * width + head_dim, head_dim),
        vector_share(width, width),
        share_mlp[0],
        share_mlp[1],
        share_mlp[2].T,
    )


def solution(mesh):
    block_count, tensor_count = mesh.devices.shape
    split = Mesh(
        mesh.devices.reshape(block_count // 2, 2, tensor_count // 2, 2), BLOCKS + TENSORS
    )
    row_weight = P(BLOCKS, TENSORS)
    column_weight = P(TENSORS, BLOCKS)
    tokens = P(None, BLOCKS, None)
    vector = P(BLOCKS)
    weights = (
        vector,
        row_weight,
        row_weight,
        row_weight,
        column_weight,
        vector,
        vector,
        vector,
        row_weight,
        row_weight,
        column_weight,
    )
    return jax.shard_map(
        local,
        mesh=split,
        in_specs=(tokens, tokens) + weights,
        out_specs=(tokens, tokens) + weights,
        check_vma=False,
    )
```

```python
import functools

import jax
import jax.numpy as jnp
from jax import lax
from jax.experimental import pallas as pl
from jax.experimental.layout import Layout, with_layout_constraint
from jax.experimental.pallas import tpu as pltpu
from jax.sharding import Mesh
from jax.sharding import PartitionSpec as P

EPSILON = 1e-06
ROTARY_BASE = 1000000.0
BF16 = jnp.bfloat16
F32 = jnp.float32
BLOCKS = ("bo", "bi")
TENSORS = ("to", "ti")
HIDDEN_CHUNK = 768
VMEM_LIMIT = 48 * 1024 * 1024


def normed(values, gain):
    return values * lax.rsqrt(jnp.mean(values * values, axis=-1, keepdims=True) + EPSILON) * gain


def rotation_tables(positions, head_dim):
    half = head_dim // 2
    inverse = jnp.power(F32(ROTARY_BASE), -(jnp.arange(half, dtype=F32) * 2.0 / head_dim))
    angles = positions.astype(F32)[:, None] * inverse[None, :]
    cosine, sine = jnp.cos(angles), jnp.sin(angles)
    return jnp.concatenate([cosine, cosine], -1), jnp.concatenate([-sine, sine], -1)


def after(array, *earlier):
    if not earlier:
        return array
    return lax.optimization_barrier((array,) + earlier)[0]


def together(arrays, earlier):
    arrays = tuple(arrays)
    if not earlier:
        return arrays
    return tuple(lax.optimization_barrier(arrays + tuple(earlier))[: len(arrays)])


def shifted(array, axis, step):
    count = lax.axis_size(axis)
    return lax.ppermute(array, axis, [(i, (i + step) % count) for i in range(count)])


def swapped(array, axis, distance=1):
    count = lax.axis_size(axis)
    return lax.ppermute(array, axis, [(i, i ^ distance) for i in range(count)])


def pick(array, index, dimension=0):
    return lax.dynamic_index_in_dim(array, index, dimension, keepdims=False)


def paired(own, other, first, dimension):
    return jnp.where(
        first, jnp.stack([own, other], dimension), jnp.stack([other, own], dimension)
    )


def gather_axis(array, axis, dimension=0):
    count = lax.axis_size(axis)
    index = lax.axis_index(axis)
    if count == 2:
        return paired(array, swapped(array, axis), index == 0, dimension)
    shape = array.shape[:dimension] + (count,) + array.shape[dimension:]
    whole = jnp.zeros(shape, array.dtype)
    for step in range(count):
        piece = array if step == 0 else shifted(array, axis, step)
        whole = lax.dynamic_update_index_in_dim(
            whole, piece, (index + count - step) % count, dimension
        )
    return whole


class Chain:
    def __init__(self):
        self.done = []

    def swap(self, arrays, distances, before=(), during=()):
        before = tuple(a for some in before for a in some) + (self.done[-2] if len(self.done) > 1 else ())
        arrays = together(arrays, before)
        arrived = tuple(swapped(a, "to", d) for a, d in zip(arrays, distances))
        arrived = together(arrived, tuple(a for some in during for a in some))
        self.done.append(arrived)
        return arrived


def sum_rows(chain, first_kept, first_sent, second_kept, second_sent, before=(), during=()):
    count = lax.axis_size("to")
    index = lax.axis_index("to")
    rows, width = first_kept.shape
    shard = 2 * rows // count
    near, far = 1, count // 2
    while True:
        arrived = chain.swap((first_sent, second_sent), (near, far), before[:1], during[:1])
        before, during = before[1:], during[1:]
        near, far = 2 * near, far // 2
        yield
        if far < 1:
            return first_kept, arrived[0], second_kept, arrived[1]
        first = first_kept + arrived[0].astype(F32)
        second = second_kept + arrived[1].astype(F32)
        bit = lax.rem(index // near, 2)
        view = first.reshape(-1, 2, shard, width)
        first_sent = pick(view, 1 - bit, 1).astype(BF16).reshape(-1, width)
        first_kept = pick(view, bit, 1).reshape(-1, width)
        bit = lax.rem(index // far, 2)
        view = second.reshape(2, -1, width)
        second_sent = pick(view, 1 - bit).astype(BF16)
        second_kept = pick(view, bit)


def gather_rows(chain, shard, before=(), during=(), vector=None):
    before = tuple(before)
    count = lax.axis_size("to")
    index = lax.axis_index("to")
    rows = shard.shape[0]
    width = shard.shape[1] // 2
    first, second = shard[None, :, :width], shard[None, :, width:]
    far, near = count // 2, 1
    while far >= 1:
        arrays, distances = (first, second), (far, near)
        if vector is not None:
            arrays, distances = arrays + (vector,), distances + (near,)
        arrived = chain.swap(arrays, distances, before[:1], during[:1])
        before, during = before[1:], during[1:]
        if vector is not None:
            vector = vector + arrived[2]
        first = paired(first, arrived[0], lax.rem(index // far, 2) == 0, 1)
        second = paired(second, arrived[1], lax.rem(index // near, 2) == 0, 0)
        first = first.reshape(-1, rows, width)
        second = second.reshape(-1, rows, width)
        far, near = far // 2, 2 * near
        yield
    whole = jnp.concatenate([first.reshape(-1, width), second.reshape(-1, width)], axis=-1)
    return whole if vector is None else (whole, vector)


def gather_parts(chain, first, second, before=()):
    first, second = first[None], second[None]
    far, near = lax.axis_size("to") // 2, 1
    while True:
        arrived = chain.swap((first, second), (far, near), before[:1])
        before = before[1:]
        far, near = far // 2, 2 * near
        yield
        if far < 1:
            return first, arrived[0], second, arrived[1]
        first = jnp.concatenate([first, arrived[0]])
        second = jnp.concatenate([second, arrived[1]])


def gather_masks(count):
    orders = []
    for distances in (lambda i: count >> (i + 1), lambda i: 1 << i):
        masks = [0]
        for i in range(count.bit_length() - 1):
            masks += [mask | distances(i) for mask in masks]
        orders.append(masks)
    return orders


def run(*stages):
    results = [None] * len(stages)
    left = dict(enumerate(stages))
    while left:
        for index in list(left):
            try:
                next(left[index])
            except StopIteration as end:
                results[index] = end.value
                del left[index]
    return results


def sum_over(vector, axes):
    for axis in axes:
        distance = 1
        while distance < lax.axis_size(axis):
            vector = vector + swapped(vector, axis, distance)
            distance *= 2
    return vector


def over_pair(array, late=()):
    return jnp.concatenate([array, after(swapped(array, "ti"), *late)], axis=-1)


def over_blocks(array, late=()):
    count = lax.axis_size("bo")
    arrived = [after(shifted(array, "bo", step), *late) for step in range(1, count)]
    return jnp.stack([array] + arrived)


def over_cores(array):
    return array, swapped(array, "bi")


LOW, HIGH, INNER, FIRST, OUTER, PLACES = 0, 1, 2, 3, 4, 5


def mxu(left, right):
    return jnp.dot(left, right, preferred_element_type=F32)


def mxu_back(left, right):
    return lax.dot_general(left, right, (((1,), (1,)), ((), ())), preferred_element_type=F32)


def mxu_outer(left, right):
    return lax.dot_general(left, right, (((0,), (0,)), ((), ())), preferred_element_type=F32)


def columns(info, position, size):
    if info is None:
        return slice(position * size, (position + 1) * size)
    return pl.ds(pl.multiple_of(info[PLACES + position] * size, 128), size)


def project(info, rows_ref, *weights):
    blocks = [(ref, i) for ref in weights for i in range(ref.shape[0])]
    total = None
    for position, (ref, i) in enumerate(blocks):
        term = mxu(rows_ref[:, columns(info, position, ref.shape[1])], ref[i])
        total = term if total is None else total + term
    return total


def project_back(grads, position, *weights):
    blocks = [(ref, i) for ref in weights for i in range(ref.shape[0])]
    ref, i = blocks[position]
    return mxu_back(grads, ref[i])


def write_halves(info, counts, total_ref, outputs, place=0):
    first_kept, first_sent, second_kept, second_sent = outputs
    rows, width = total_ref.shape
    shard, middle = rows // counts, width // 2
    for j in range(counts // 2):
        for target, bit in ((first_kept, info[LOW]), (first_sent, 1 - info[LOW])):
            source = pl.ds(pl.multiple_of((2 * j + bit) * shard, shard), shard)
            target[j, place] = total_ref[source, :middle].astype(target.dtype)
        for target, bit in ((second_kept, info[HIGH]), (second_sent, 1 - info[HIGH])):
            source = pl.ds(pl.multiple_of((bit * (counts // 2) + j) * shard, shard), shard)
            target[j, place] = total_ref[source, middle:].astype(target.dtype)


def read_parts(info, counts, parts, target):
    rows, width = target.shape
    shard, middle = rows // counts, width // 2
    for side, masks in enumerate(gather_masks(counts)):
        for i, mask in enumerate(masks):
            ref = parts[2 * side + 2 * i // counts]
            place = pl.multiple_of(jnp.bitwise_xor(info[OUTER], mask) * shard, shard)
            columns_now = slice(side * middle, (side + 1) * middle)
            target[pl.ds(place, shard), columns_now] = ref[i % (counts // 2), 0]


def unit(values):
    return lax.rsqrt(jnp.mean(values * values, axis=-1, keepdims=True) + EPSILON)


def swap_halves(values):
    return pltpu.roll(values, values.shape[-1] // 2, 1)


def prepare_kernel(
    sizes,
    info,
    x_ref,
    gain_ref,
    query_gain_ref,
    key_gain_ref,
    cosine_ref,
    sine_ref,
    query_mine,
    query_theirs,
    kv_mine,
    kv_theirs,
    normal_ref,
    query_raw_ref,
    key_raw_ref,
    query_ref,
    kv_ref,
):
    head_dim, pair_heads, key_heads = sizes
    x = x_ref[0].astype(F32)
    normal_ref, query_raw_ref, key_raw_ref, query_ref, kv_ref = (
        ref.at[0] for ref in (normal_ref, query_raw_ref, key_raw_ref, query_ref, kv_ref)
    )
    normal_ref[...] = (x * unit(x) * gain_ref[...]).astype(BF16)
    cosine, sine = cosine_ref[...], sine_ref[...]

    def rotated(raw, gain):
        values = raw * unit(raw) * gain
        return (values * cosine + swap_halves(values) * sine).astype(BF16)

    query_raw = project(info, normal_ref, query_mine, query_theirs)
    query_raw_ref[...] = query_raw
    for head in range(query_raw.shape[1] // head_dim):
        part = slice(head * head_dim, (head + 1) * head_dim)
        query_ref[:, part] = rotated(query_raw[:, part], query_gain_ref[...])
    kv_raw = project(info, normal_ref, kv_mine, kv_theirs)
    for head in range(pair_heads):
        start = (2 * key_heads * (head // key_heads) + head % key_heads) * head_dim
        raw = kv_raw[:, start : start + head_dim]
        key_raw_ref[:, head * head_dim : (head + 1) * head_dim] = raw
        kv_ref[0, head] = rotated(raw, key_gain_ref[...])
        start += key_heads * head_dim
        kv_ref[1, head] = kv_raw[:, start : start + head_dim].astype(BF16)


def row_sums(parts):
    first_kept, first_arrived, second_kept, second_arrived = (ref[...] for ref in parts)
    return jnp.concatenate(
        [first_kept + first_arrived.astype(F32), second_kept + second_arrived.astype(F32)], axis=-1
    )


def norm_back(grad, values, gain):
    scale = unit(values)
    inner = grad * gain
    mean = jnp.mean(inner * values, axis=-1, keepdims=True)
    term = jnp.sum(grad * values * scale, axis=0, keepdims=True)
    return scale * inner - values * (scale * scale * scale * mean), term


def residual_kernel(x_ref, gain_ref, *refs):
    residual_ref, first_ref, second_ref = refs[4:]
    residual = x_ref[...].astype(F32) + row_sums(refs[:4])
    residual_ref[...] = residual
    normal = (residual * unit(residual) * gain_ref[...]).astype(BF16)
    middle = normal.shape[1] // 2
    first_ref[...] = normal[:, :middle]
    second_ref[...] = normal[:, middle:]


def residual_back_kernel(groups, residual_ref, grad_out_ref, gain_ref, *refs):
    layer_ref, grad_ref, first_ref, second_ref, term_ref = refs[4 * groups :]
    shard = residual_ref.shape[0] // groups
    middle = residual_ref.shape[1] // 2
    total = jnp.zeros(term_ref.shape, F32)
    for group in range(groups):
        place = slice(group * shard, (group + 1) * shard)
        sums = row_sums(refs[4 * group : 4 * group + 4])
        residual = residual_ref[place, :]
        layer_ref[place, :] = (residual + sums[shard:]).astype(BF16)
        grad, term = norm_back(sums[:shard], residual, gain_ref[...])
        grad += grad_out_ref[place, :].astype(F32)
        total += term
        grad_ref[place, :] = grad
        first_ref[place, :] = grad[:, :middle].astype(BF16)
        second_ref[place, :] = grad[:, middle:].astype(BF16)
    term_ref[...] = total


def hidden_kernel(x_ref, gain_ref, grad_residual_ref, *refs):
    hidden_ref, term_ref = refs[4:]
    grad, term = norm_back(row_sums(refs[:4]), x_ref[...].astype(F32), gain_ref[...])
    hidden_ref[...] = (grad_residual_ref[...] + grad).astype(BF16)
    term_ref[...] = term


def visible_scores(info, queries, keys, position, blocks, rows, scale):
    scores = mxu_back(queries, keys) * scale
    if position == 0:
        query_rows = lax.broadcasted_iota(jnp.int32, scores.shape, 0) % rows
        key_rows = lax.broadcasted_iota(jnp.int32, scores.shape, 1)
        return jnp.where(key_rows <= query_rows, scores, -jnp.inf)
    return jnp.where(info[PLACES + blocks + position] > 0, scores, -jnp.inf)


def attend_kernel(
    sizes,
    info,
    query_ref,
    kv_mine,
    kv_theirs,
    out_mine,
    out_theirs,
    attn_ref,
    log_ref,
    attended_ref,
    first_kept,
    first_sent,
    second_kept,
    second_sent,
    scores_ref,
    total_ref,
):
    head_dim, pair_heads, group, counts = sizes
    query_ref, attn_ref, log_ref, attended_ref = (
        ref.at[0] for ref in (query_ref, attn_ref, log_ref, attended_ref)
    )
    rows = query_ref.shape[0]
    half = kv_mine.shape[0]
    scale = head_dim ** (-0.5)
    lanes = lax.broadcasted_iota(jnp.int32, (rows, head_dim), 1)
    logs = jnp.zeros((rows, head_dim), F32)

    def key_value(which, position, head):
        ref = kv_mine if position < half else kv_theirs
        return ref[position % half, 0, which, head]

    for head in range(pair_heads):
        queries = jnp.concatenate(
            [
                query_ref[:, (head * group + i) * head_dim : (head * group + i + 1) * head_dim]
                for i in range(group)
            ]
        )
        top = None
        for position in range(2 * half):
            scores = visible_scores(
                info, queries, key_value(0, position, head), position, 2 * half, rows, scale
            )
            scores_ref[position] = scores
            block_top = jnp.max(scores, axis=-1, keepdims=True)
            top = block_top if top is None else jnp.maximum(top, block_top)
        total = jnp.zeros_like(top)
        weighted = jnp.zeros((group * rows, head_dim), F32)
        for position in range(2 * half):
            weights = jnp.exp(scores_ref[position] - top)
            total += jnp.sum(weights, axis=-1, keepdims=True)
            weighted += mxu(weights.astype(BF16), key_value(1, position, head))
        attn = weighted / total
        log_total = top + jnp.log(total)
        for i in range(group):
            index = head * group + i
            part = slice(index * head_dim, (index + 1) * head_dim)
            piece = attn[i * rows : (i + 1) * rows]
            attn_ref[:, part] = piece
            attended_ref[:, part] = piece.astype(BF16)
            logs = jnp.where(lanes == index, log_total[i * rows : (i + 1) * rows], logs)
    log_ref[...] = logs
    attended = attended_ref[...]
    for position in range(2 * half):
        total_ref[:, columns(info, position, out_mine.shape[1])] = project_back(
            attended, position, out_mine, out_theirs
        )
    write_halves(info, counts, total_ref, (first_kept, first_sent, second_kept, second_sent))


def feed_forward_kernel(
    counts,
    info,
    first_own,
    first_other,
    second_own,
    second_other,
    grad_ref,
    gate_ref,
    up_ref,
    down_ref,
    active_ref,
    grad_gate_ref,
    grad_up_ref,
    mid_ref,
    *outputs,
):
    grad_total, mlp_total = outputs[4:]
    step = pl.program_id(0)

    @pl.when(step == 0)
    def _():
        read_parts(info, counts, (first_own, first_other, second_own, second_other), mid_ref)

    blocks, size = gate_ref.shape[0], gate_ref.shape[1]
    gate = project(None, mid_ref, gate_ref)
    up = project(None, mid_ref, up_ref)
    grad = project(None, grad_ref.at[0], down_ref)
    slope = jax.nn.sigmoid(gate)
    silu = gate * slope
    active = (silu * up).astype(BF16)
    grad_gate = (grad * up * slope * (1.0 + gate * (1.0 - slope))).astype(BF16)
    grad_up = (grad * silu).astype(BF16)
    active_ref[...] = active
    grad_gate_ref[...] = grad_gate
    grad_up_ref[...] = grad_up

    def term(position):
        part = columns(None, position, size)
        grad_term = project_back(grad_gate, position, gate_ref) + project_back(
            grad_up, position, up_ref
        )
        return part, grad_term, project_back(active, position, down_ref)

    @pl.when(step == 0)
    def _():
        for position in range(blocks):
            part, grad_term, mlp_term = term(position)
            grad_total[:, part] = grad_term
            mlp_total[:, part] = mlp_term

    @pl.when(step > 0)
    def _():
        for position in range(blocks):
            part, grad_term, mlp_term = term(position)
            grad_total[:, part] += grad_term
            mlp_total[:, part] += mlp_term

    @pl.when(step == pl.num_programs(0) - 1)
    def _():
        write_halves(info, counts, grad_total, outputs[:4], 0)
        write_halves(info, counts, mlp_total, outputs[:4], 1)


def attend_back_kernel(
    sizes,
    info,
    first_own,
    first_other,
    second_own,
    second_other,
    out_mine,
    out_theirs,
    query_ref,
    kv_mine,
    kv_theirs,
    attn_ref,
    log_ref,
    branch_ref,
    grad_query_ref,
    kept_ref,
    sent_ref,
):
    head_dim, pair_heads, group, counts = sizes
    query_ref, attn_ref, log_ref, branch_ref, grad_query_ref = (
        ref.at[0] for ref in (query_ref, attn_ref, log_ref, branch_ref, grad_query_ref)
    )
    read_parts(info, counts, (first_own, first_other, second_own, second_other), branch_ref)
    rows = query_ref.shape[0]
    half = kv_mine.shape[0]
    scale = head_dim ** (-0.5)
    grad_attended = project(info, branch_ref, out_mine, out_theirs).astype(BF16)

    def key_value(which, position, head):
        ref = kv_mine if position < half else kv_theirs
        return ref[position % half, 0, which, head]

    for head in range(pair_heads):
        parts = [
            slice((head * group + i) * head_dim, (head * group + i + 1) * head_dim)
            for i in range(group)
        ]
        queries = jnp.concatenate([query_ref[:, part] for part in parts])
        grads = jnp.concatenate([grad_attended[:, part] for part in parts])
        attn = jnp.concatenate([attn_ref[:, part] for part in parts])
        logs = jnp.concatenate(
            [log_ref[:, head * group + i : head * group + i + 1] for i in range(group)]
        )
        row_dots = jnp.sum(grads.astype(F32) * attn, axis=-1, keepdims=True)
        grad_query = jnp.zeros((group * rows, head_dim), F32)
        for position in range(2 * half):
            keys = key_value(0, position, head)
            scores = visible_scores(info, queries, keys, position, 2 * half, rows, scale)
            probs = jnp.exp(scores - logs)
            grad_probs = mxu_back(grads, key_value(1, position, head))
            grad_scores = (probs * (grad_probs - row_dots) * scale).astype(BF16)
            grad_query += mxu(grad_scores, keys)
            target = kept_ref if position < half else sent_ref
            target[position % half, 0, 0, head] = mxu_outer(grad_scores, queries).astype(target.dtype)
            target[position % half, 0, 1, head] = mxu_outer(probs.astype(BF16), grads).astype(
                target.dtype
            )
        for i, part in enumerate(parts):
            grad_query_ref[:, part] = grad_query[i * rows : (i + 1) * rows]


def finish_kernel(
    sizes,
    info,
    grad_query_ref,
    query_raw_ref,
    key_raw_ref,
    shares_ref,
    query_gain_ref,
    key_gain_ref,
    cosine_ref,
    sine_ref,
    query_mine,
    query_theirs,
    kv_mine,
    kv_theirs,
    query_low_ref,
    kv_low_ref,
    gains_ref,
    first_kept,
    first_sent,
    second_kept,
    second_sent,
    total_ref,
):
    head_dim, pair_heads, key_heads, counts = sizes
    grad_query_ref, query_raw_ref, key_raw_ref, shares_ref, query_low_ref, kv_low_ref, gains_ref = (
        ref.at[0]
        for ref in (
            grad_query_ref,
            query_raw_ref,
            key_raw_ref,
            shares_ref,
            query_low_ref,
            kv_low_ref,
            gains_ref,
        )
    )
    cosine, sine = cosine_ref[...], sine_ref[...]

    def back(grad, raw, gain):
        grad = grad * cosine - swap_halves(grad) * sine
        scale = unit(raw)
        gain_term = jnp.sum(grad * raw * scale, axis=0, keepdims=True)
        inner = grad * gain
        mean = jnp.mean(inner * raw, axis=-1, keepdims=True)
        return (scale * inner - raw * (scale * scale * scale * mean)).astype(BF16), gain_term

    total = jnp.zeros((1, head_dim), F32)
    for head in range(query_raw_ref.shape[1] // head_dim):
        part = slice(head * head_dim, (head + 1) * head_dim)
        query_low_ref[:, part], term = back(
            grad_query_ref[:, part], query_raw_ref[:, part], query_gain_ref[...]
        )
        total += term
    gains_ref[0:1, :] = total
    total = jnp.zeros((1, head_dim), F32)
    for head in range(pair_heads):
        start = (2 * key_heads * (head // key_heads) + head % key_heads) * head_dim
        kv_low_ref[:, start : start + head_dim], term = back(
            shares_ref[0, head],
            key_raw_ref[:, head * head_dim : (head + 1) * head_dim],
            key_gain_ref[...],
        )
        total += term
        start += key_heads * head_dim
        kv_low_ref[:, start : start + head_dim] = shares_ref[1, head].astype(BF16)
    gains_ref[1:2, :] = total
    query_low, kv_low = query_low_ref[...], kv_low_ref[...]
    for position in range(2 * query_mine.shape[0]):
        total_ref[:, columns(info, position, query_mine.shape[1])] = project_back(
            query_low, position, query_mine, query_theirs
        ) + project_back(kv_low, position, kv_mine, kv_theirs)
    write_halves(info, counts, total_ref, (first_kept, first_sent, second_kept, second_sent))


def weight_kernel(counts, products, info, *refs):
    arrays, start = [], 0
    for count in counts:
        arrays.append(refs[start : start + count])
        start += count
    out_ref = refs[-1]

    def rows_of(members):
        flat = [ref[...].reshape(-1, ref.shape[-1]) for ref in members]
        return flat[0] if len(flat) == 1 else jnp.concatenate(flat)

    place = 0
    for left, rights in products:
        left_rows = rows_of(arrays[left])
        for right in rights:
            total = mxu_outer(left_rows, rows_of(arrays[right])).astype(BF16)
            if len(out_ref.shape) == 5:
                out_ref[0, 0, place] = total
                place += 1
            else:
                out_ref[0, 0, :, place : place + total.shape[1]] = total
                place += total.shape[1]


def whole_spec(dims):
    return pl.BlockSpec(dims, lambda i, info: (0,) * len(dims))


def group_spec(array, dimension=0):
    dims = array.shape[:dimension] + (1,) + array.shape[dimension + 1 :]
    rest = len(dims) - dimension - 1
    return pl.BlockSpec(dims, lambda g, info: (0,) * dimension + (g,) + (0,) * rest)


def plain_call(kernel, operands, outputs):
    moved = sum(a.size * a.dtype.itemsize for a in tuple(operands) + tuple(outputs))
    return pl.pallas_call(
        kernel,
        out_shape=tuple(outputs),
        compiler_params=pltpu.CompilerParams(vmem_limit_bytes=VMEM_LIMIT),
        cost_estimate=pl.CostEstimate(flops=0, bytes_accessed=moved, transcendentals=0),
    )(*operands)


def group_call(kernel, groups, info, operands, outputs, scratch=(), flops=0):
    moved = sum(a.size * a.dtype.itemsize for a, _ in tuple(operands) + tuple(outputs))
    return pl.pallas_call(
        kernel,
        out_shape=[a for a, _ in outputs],
        grid_spec=pltpu.PrefetchScalarGridSpec(
            num_scalar_prefetch=1,
            grid=(groups,),
            in_specs=[spec for _, spec in operands],
            out_specs=[spec for _, spec in outputs],
            scratch_shapes=list(scratch),
        ),
        compiler_params=pltpu.CompilerParams(vmem_limit_bytes=VMEM_LIMIT),
        cost_estimate=pl.CostEstimate(flops=flops, bytes_accessed=moved, transcendentals=0),
    )(info, *[a for a, _ in operands])


def shape(dims, dtype):
    return jax.ShapeDtypeStruct(dims, dtype)


def weight_blocks(info, lefts, rights, products, blocks, pair, stacked, in_order):
    width = lefts[0][0].shape[-1]
    size = width // blocks
    batch_rows = sum(a.shape[0] for a in lefts[0]) if lefts[0][0].ndim == 2 else None
    operands, specs = [], []
    for array in [a for members in lefts for a in members]:
        operands.append(array)
        if array.ndim == 2:
            spec = pl.BlockSpec((array.shape[0], size), lambda t, b, info: (0, b))
        elif array.shape[0] * array.shape[1] == batch_rows or batch_rows is None:
            spec = pl.BlockSpec(array.shape[:2] + (size,), lambda t, b, info: (0, 0, b))
        else:
            spec = pl.BlockSpec(
                (array.shape[0] // pair, array.shape[1], size),
                lambda t, b, info: (info[INNER], 0, b),
            )
        specs.append(spec)
    widths = []
    for members in rights:
        widths.append(members[0].shape[-1] // pair)
        for array in members:
            operands.append(array)
            dims = array.shape[:-1] + (array.shape[-1] // pair,)
            zeros = (0,) * (array.ndim - 1)
            specs.append(
                pl.BlockSpec(
                    dims,
                    lambda t, b, info, zeros=zeros: zeros
                    + (t if in_order else lax.rem(t + info[INNER], 2),),
                )
            )
    if stacked:
        dims = (pair, blocks, len(rights), size, widths[0])
        out_spec = pl.BlockSpec((1, 1) + dims[2:], lambda t, b, info: (t, b, 0, 0, 0))
    else:
        dims = (pair, blocks, size, sum(widths))
        out_spec = pl.BlockSpec((1, 1) + dims[2:], lambda t, b, info: (t, b, 0, 0))
    counts = [len(members) for members in tuple(lefts) + tuple(rights)]
    placed = [(left, [len(lefts) + right for right in columns_of]) for left, columns_of in products]
    rows = rights[0][0].size * len(rights[0]) // rights[0][0].shape[-1]
    flops = 2 * rows * width * pair * sum(widths)
    moved = 2 * pair * width * sum(widths)
    return pl.pallas_call(
        functools.partial(weight_kernel, counts, placed),
        out_shape=shape(dims, BF16),
        grid_spec=pltpu.PrefetchScalarGridSpec(
            num_scalar_prefetch=1,
            grid=(pair, blocks),
            in_specs=specs,
            out_specs=out_spec,
        ),
        compiler_params=pltpu.CompilerParams(vmem_limit_bytes=VMEM_LIMIT),
        cost_estimate=pl.CostEstimate(flops=flops, bytes_accessed=moved, transcendentals=0),
    )(info, *operands)


def local(
    hidden_in,
    out_grad,
    norm_in,
    w_query,
    key_weight,
    value_weight,
    w_out,
    query_gain,
    key_gain,
    norm_mid,
    w_gate,
    w_up,
    w_down,
):
    block_outers = lax.axis_size("bo")
    blocks = block_outers * lax.axis_size("bi")
    block_outer = lax.axis_index("bo")
    block_inner = lax.axis_index("bi")
    block = block_outer * lax.axis_size("bi") + block_inner
    outer = lax.axis_index("to")
    inner = lax.axis_index("ti")
    pair = lax.axis_size("ti")
    counts = lax.axis_size("to")
    batch, rows, width = hidden_in.shape
    head_dim = query_gain.shape[0] * blocks
    query_width = w_query.shape[1]
    key_width = key_weight.shape[1]
    hidden_units = w_gate.shape[1]
    key_heads = key_width // head_dim
    query_heads = query_width * pair // head_dim
    pair_heads = key_heads * pair
    group_size = query_heads // pair_heads
    shard_rows = rows // counts

    query_half = over_pair(w_query)
    kv_half = over_blocks(jnp.concatenate([key_weight, value_weight], axis=1))
    query_most = over_blocks(query_half)
    kv_most = over_pair(kv_half)
    query_full = over_cores(query_most)
    kv_full = over_cores(kv_most)
    out_half = over_blocks(after(w_out.T, query_half))
    mlp_own = jnp.concatenate([w_gate, w_up, w_down.T], axis=1)

    own_gains = jnp.concatenate([norm_in, norm_mid, query_gain, key_gain])[None]
    own_gains = after(own_gains, kv_half)
    all_gains = gather_axis(gather_axis(own_gains, "bo"), "bi", 1)
    all_gains = all_gains.reshape(blocks, -1).astype(F32)
    part = norm_in.shape[0]
    gain_in = all_gains[:, :part].reshape(-1)
    gain_mid = all_gains[:, part : 2 * part].reshape(-1)
    head_part = query_gain.shape[0]
    gain_query = all_gains[:, 2 * part : 2 * part + head_part].reshape(1, -1)
    gain_key = all_gains[:, 2 * part + head_part :].reshape(1, -1)

    positions = block * rows + jnp.arange(rows, dtype=jnp.int32)
    cosine, sine = rotation_tables(positions, head_dim)
    block_ids = []
    for side in range(2):
        side_inner = block_inner if side == 0 else 1 - block_inner
        for step in range(block_outers):
            owner = lax.rem(block_outer + block_outers - step, block_outers)
            block_ids.append(owner * 2 + side_inner)
    groups = batch // pair
    first_sequence = inner * groups
    info = jnp.stack(
        [lax.rem(outer, 2), outer // (counts // 2), inner, first_sequence, outer]
        + block_ids
        + [(b < block).astype(jnp.int32) for b in block_ids]
    ).astype(jnp.int32)

    chain = Chain()
    all_heads = query_heads * head_dim
    all_keys = pair_heads * head_dim
    kv_dims = (groups, 2, pair_heads, rows, head_dim)
    side_dims = (block_outers,) + kv_dims
    half_dims = (counts // 2, groups, shard_rows, width // 2)
    whole_rows = pltpu.VMEM((rows, width), F32)

    def by_group(dims, dtype, dimension=0):
        array = shape(dims, dtype)
        return array, group_spec(array, dimension)

    def per_group(*arrays):
        return tuple((a, group_spec(a)) for a in arrays)

    def per_second(*arrays):
        return tuple((a, group_spec(a, 1)) for a in arrays)

    def shared(*arrays):
        return tuple((a, whole_spec(a.shape)) for a in arrays)

    halves = (by_group(half_dims, F32, 1), by_group(half_dims, BF16, 1)) * 2

    def flat(parts):
        return [part.reshape(-1, part.shape[-1]) for part in parts]

    def own_sequences(array):
        return (array, pl.BlockSpec((1, rows, width), lambda g, info: (info[FIRST] + g, 0, 0)))

    normal_in, query_raw, key_raw, query_rows, kv_rows = group_call(
        functools.partial(prepare_kernel, (head_dim, pair_heads, key_heads)),
        groups,
        info,
        (own_sequences(hidden_in),)
        + shared(after(gain_in[None], out_half), gain_query, gain_key, cosine, sine)
        + shared(*query_full, *kv_full),
        (
            by_group((groups, rows, width), BF16),
            by_group((groups, rows, all_heads), F32),
            by_group((groups, rows, all_keys), F32),
            by_group((groups, rows, all_heads), BF16),
            by_group(kv_dims, BF16),
        ),
        flops=2 * groups * rows * width * (all_heads + 2 * all_keys),
    )
    mlp_own = with_layout_constraint(after(mlp_own, query_rows), Layout((0, 1)))
    mlp_weights = lax.all_gather(mlp_own, ("ti", "bo", "bi"), axis=0)
    kv_blocks = over_blocks(kv_rows)
    key_value = over_cores(kv_blocks)
    out_full = over_cores(over_pair(out_half, (kv_blocks,)))
    attn, log_total, attended, *out_parts = group_call(
        functools.partial(attend_kernel, (head_dim, pair_heads, group_size, counts)),
        groups,
        info,
        per_group(query_rows) + per_second(*key_value) + shared(*out_full),
        (
            by_group((groups, rows, all_heads), F32),
            by_group((groups, rows, head_dim), F32),
            by_group((groups, rows, all_heads), BF16),
        )
        + halves,
        scratch=[pltpu.VMEM((blocks, group_size * rows, rows), F32), whole_rows],
        flops=2 * groups * rows * all_heads * (width + 4 * blocks * rows),
    )

    def own_shard(array):
        starts = (first_sequence, outer * shard_rows, 0)
        part = lax.dynamic_slice(array, starts, (groups, shard_rows, width))
        return part.reshape(-1, width)

    x_shard = own_shard(hidden_in)
    grad_out_shard = own_shard(out_grad)
    shard_dims = (groups * shard_rows, width)
    half_shard = shape((groups * shard_rows, width // 2), BF16)
    (sums,) = run(sum_rows(chain, *flat(out_parts)))
    residual, *normal_mid = plain_call(
        residual_kernel,
        (x_shard, gain_mid[None]) + sums,
        (shape(shard_dims, F32), half_shard, half_shard),
    )
    normal_mid = [half.reshape(groups, shard_rows, -1) for half in normal_mid]
    mid_parts = []
    for group in range(groups):
        mid_parts += run(gather_parts(chain, *(half[group] for half in normal_mid)))

    chunks = pair * hidden_units // HIDDEN_CHUNK
    steps = hidden_units // HIDDEN_CHUNK
    weight_dims = (blocks, width // blocks, HIDDEN_CHUNK)

    def weight_spec(place):
        return pl.BlockSpec(
            weight_dims, lambda i, info: (i // steps, 0, place * steps + lax.rem(i, steps))
        )

    piece = pl.BlockSpec((rows, HIDDEN_CHUNK), lambda i, info: (0, i))
    hidden_shape = shape((rows, pair * hidden_units), BF16)
    one_dims = (counts // 2, 1, shard_rows, width // 2)
    two_dims = (counts // 2, 2, shard_rows, width // 2)
    two_halves = (shape(two_dims, F32), shape(two_dims, BF16)) * 2
    mid, active, grad_gate, grad_up, mlp_parts = [], [], [], [], []
    for group in range(groups):
        parts = [part.reshape(one_dims) for part in mid_parts[group]]
        sequence = pl.BlockSpec(
            (1, rows, width), lambda i, info, group=group: (info[FIRST] + group, 0, 0)
        )
        results = pl.pallas_call(
            functools.partial(feed_forward_kernel, counts),
            out_shape=(hidden_shape,) * 3 + (shape((rows, width), BF16),) + two_halves,
            grid_spec=pltpu.PrefetchScalarGridSpec(
                num_scalar_prefetch=1,
                grid=(chunks,),
                in_specs=[whole_spec(one_dims)] * 4 + [sequence] + [weight_spec(i) for i in range(3)],
                out_specs=(piece,) * 3 + (whole_spec((rows, width)),) + (whole_spec(two_dims),) * 4,
                scratch_shapes=[whole_rows] * 2,
            ),
            compiler_params=pltpu.CompilerParams(vmem_limit_bytes=VMEM_LIMIT),
            cost_estimate=pl.CostEstimate(
                flops=12 * rows * width * pair * hidden_units,
                bytes_accessed=6 * width * pair * hidden_units,
                transcendentals=rows * pair * hidden_units,
            ),
        )(info, *parts, out_grad, mlp_weights, mlp_weights, mlp_weights)
        active.append(results[0])
        grad_gate.append(results[1])
        grad_up.append(results[2])
        mid.append(results[3])
        mlp_parts.append(results[4:])

    both_sums = []
    first_arrived = ()
    for group in range(groups - 1):
        mark = len(chain.done)
        both_sums += run(sum_rows(chain, *flat(mlp_parts[group]), during=((active[-1],),)))
        first_arrived = chain.done[mark]
    mlp_terms = weight_blocks(
        after(info, *first_arrived),
        (mid, [out_grad]),
        (grad_gate, grad_up, active),
        [(0, [0, 1]), (1, [2])],
        blocks,
        pair,
        True,
        True,
    )
    both_sums += run(sum_rows(chain, *flat(mlp_parts[-1]), during=((mlp_terms,),)))
    last_arrived = chain.done[-1]
    layer_shard, grad_residual, *branch_halves, gain_mid_term = plain_call(
        functools.partial(residual_back_kernel, groups),
        (residual, grad_out_shard, gain_mid[None]) + tuple(a for sums in both_sums for a in sums),
        (
            shape(shard_dims, BF16),
            shape(shard_dims, F32),
            half_shard,
            half_shard,
            shape((1, width), F32),
        ),
    )

    half_groups = groups // 2

    def in_order(own, arrived):
        return paired(own, arrived, inner == 0, 0)

    layer_shard = layer_shard.reshape(groups, shard_rows, width)
    late = layer_shard[half_groups:].reshape(-1, width)
    late_arrived = swapped(late, "ti")
    late = in_order(late, late_arrived).reshape(-1, width)
    early_rows = half_groups * shard_rows
    layer_rows = jnp.concatenate([layer_shard[:half_groups].reshape(-1, width), late])
    (branch_parts,) = run(
        gather_parts(chain, *branch_halves, ((), (late_arrived,)))
    )
    branch_parts = [part.reshape(half_dims) for part in branch_parts]
    branch, grad_query, kv_kept, kv_sent = group_call(
        functools.partial(attend_back_kernel, (head_dim, pair_heads, group_size, counts)),
        groups,
        info,
        per_second(*branch_parts)
        + shared(*out_full)
        + per_group(query_rows)
        + per_second(*key_value)
        + per_group(attn, log_total),
        (
            by_group((groups, rows, width), BF16),
            by_group((groups, rows, all_heads), F32),
            by_group(side_dims, F32, 1),
            by_group(side_dims, BF16, 1),
        ),
        flops=2 * groups * rows * all_heads * (width + 10 * blocks * rows),
    )

    kv_arrived = swapped(kv_sent, "bi")
    mine = kv_kept + kv_arrived.astype(F32)
    low = mine.astype(BF16)

    layer_chain = Chain()
    layer_stage = gather_rows(layer_chain, layer_rows, ((kv_arrived,),))
    next(layer_stage)
    layer_first = layer_chain.done[0]
    shares = mine[0]
    for step in range(1, block_outers):
        arrived = shifted(low[step], "bo", block_outers - step)
        shares += after(arrived, *layer_first).astype(F32)
    (layer_whole,) = run(layer_stage)
    layer_second = layer_chain.done[1:]
    layer_whole = layer_whole.reshape(counts, -1, width)
    layer_early = layer_whole[:, :early_rows]
    layer_arrived = swapped(layer_early, "ti")

    grad_query_low, grad_kv_low, gain_terms, *in_parts = group_call(
        functools.partial(finish_kernel, (head_dim, pair_heads, key_heads, counts)),
        groups,
        info,
        per_group(grad_query, query_raw, key_raw, shares)
        + shared(gain_query, gain_key, cosine, sine, *query_full, *kv_full),
        (
            by_group((groups, rows, all_heads), BF16),
            by_group((groups, rows, 2 * all_keys), BF16),
            by_group((groups, 2, head_dim), F32),
        )
        + halves,
        scratch=[whole_rows],
        flops=2 * groups * rows * width * (all_heads + 2 * all_keys),
    )
    attn_terms = weight_blocks(
        info,
        ([normal_in], [branch]),
        ([grad_query_low], [grad_kv_low], [attended]),
        [(0, [0, 1]), (1, [2])],
        blocks,
        pair,
        False,
        False,
    )

    in_parts = flat(in_parts)
    during = ((attn_terms,), (layer_arrived,))
    (sums,) = run(sum_rows(chain, *in_parts, before=layer_second, during=during))
    sum_arrived = chain.done[-1]
    hidden_shard, gain_in_term = plain_call(
        hidden_kernel,
        (x_shard, gain_in[None], grad_residual) + sums,
        (shape(shard_dims, BF16), shape((1, width), F32)),
    )
    hidden_shard = hidden_shard.reshape(groups, shard_rows, width)

    def weight_sum(terms):
        flat = terms.reshape((-1,) + terms.shape[-1:])
        raw = lax.psum_scatter(flat, ("ti", "bo", "bi"), scatter_dimension=0, tiled=True)
        share = with_layout_constraint(raw, Layout((0, 1)))
        return share.astype(F32).reshape(terms.shape[2:]), raw

    share_mlp, mlp_raw = weight_sum(after(mlp_terms, *last_arrived))
    share_attn, _ = weight_sum(after(attn_terms, mlp_raw, *sum_arrived))
    vectors = jnp.concatenate(
        [gain_in_term[0], gain_mid_term[0], gain_terms.sum(0).reshape(-1)]
    )
    hidden_late = hidden_shard[half_groups:].reshape(-1, width)
    hidden_arrived = swapped(hidden_late, "ti")
    vectors = vectors[None]
    vector_arrived = swapped(vectors, "ti")
    hidden_early = hidden_shard[:half_groups].reshape(-1, width)
    (hidden_early,) = run(gather_rows(chain, hidden_early, ((), (hidden_arrived,))))
    hidden_early_arrived = swapped(hidden_early, "ti")
    vectors = vectors + after(vector_arrived, *chain.done[-1])
    hidden_late = in_order(hidden_late, hidden_arrived).reshape(-1, width)
    during = ((), (hidden_early_arrived,))
    ((hidden_late, vectors),) = run(
        gather_rows(chain, hidden_late, during=during, vector=vectors)
    )
    vectors = sum_over(vectors, BLOCKS)[0]
    kv_start = query_width + 2 * key_width
    weight_grads = (
        share_attn[:, :query_width],
        share_attn[:, query_width : query_width + key_width],
        share_attn[:, query_width + key_width : kv_start],
        share_attn[:, kv_start:].T,
        share_mlp[0],
        share_mlp[1],
        share_mlp[2].T,
    )
    def assembled(early, arrived, late):
        late = late.reshape(counts, pair, groups - half_groups, shard_rows, width)
        late = late.transpose(1, 2, 0, 3, 4).reshape(pair, -1, rows, width)
        early = in_order(early, arrived).reshape(pair, counts, half_groups, shard_rows, width)
        early = early.transpose(0, 2, 1, 3, 4).reshape(pair, -1, rows, width)
        return jnp.concatenate([early, late], axis=1).reshape(batch, rows, width)

    layer_out = assembled(layer_early, layer_arrived, layer_whole[:, early_rows:])
    hidden_early_arrived = after(hidden_early_arrived, layer_out, *weight_grads)
    grad_hidden = assembled(hidden_early, hidden_early_arrived, hidden_late)

    def vector_share(first, size):
        return lax.dynamic_slice_in_dim(vectors, first + block * (size // blocks), size // blocks)

    return (
        layer_out,
        grad_hidden,
        vector_share(0, width),
        *weight_grads[:4],
        vector_share(2 * width, head_dim),
        vector_share(2 * width + head_dim, head_dim),
        vector_share(width, width),
        *weight_grads[4:],
    )


def solution(mesh):
    block_count, tensor_count = mesh.devices.shape
    split = Mesh(
        mesh.devices.reshape(block_count // 2, 2, tensor_count // 2, 2), BLOCKS + TENSORS
    )
    row_weight = P(BLOCKS, TENSORS)
    column_weight = P(TENSORS, BLOCKS)
    tokens = P(None, BLOCKS, None)
    vector = P(BLOCKS)
    weights = (
        vector,
        row_weight,
        row_weight,
        row_weight,
        column_weight,
        vector,
        vector,
        vector,
        row_weight,
        row_weight,
        column_weight,
    )
    return jax.shard_map(
        local,
        mesh=split,
        in_specs=(tokens, tokens) + weights,
        out_specs=(tokens, tokens) + weights,
        check_vma=False,
    )
```

```python
import functools

import jax
import jax.numpy as jnp
from jax import lax
from jax.experimental import pallas as pl
from jax.experimental.layout import Layout, with_layout_constraint
from jax.experimental.pallas import tpu as pltpu
from jax.sharding import Mesh
from jax.sharding import PartitionSpec as P

EPSILON = 1e-06
ROTARY_BASE = 1000000.0
BF16 = jnp.bfloat16
F32 = jnp.float32
BLOCKS = ("bo", "bi")
TENSORS = ("to", "ti")
HIDDEN_CHUNK = 768
VMEM_LIMIT = 48 * 1024 * 1024


def normed(values, gain):
    return values * lax.rsqrt(jnp.mean(values * values, axis=-1, keepdims=True) + EPSILON) * gain


def rotation_tables(positions, head_dim):
    half = head_dim // 2
    inverse = jnp.power(F32(ROTARY_BASE), -(jnp.arange(half, dtype=F32) * 2.0 / head_dim))
    angles = positions.astype(F32)[:, None] * inverse[None, :]
    cosine, sine = jnp.cos(angles), jnp.sin(angles)
    return jnp.concatenate([cosine, cosine], -1), jnp.concatenate([-sine, sine], -1)


def after(array, *earlier):
    if not earlier:
        return array
    return lax.optimization_barrier((array,) + earlier)[0]


def together(arrays, earlier):
    arrays = tuple(arrays)
    if not earlier:
        return arrays
    return tuple(lax.optimization_barrier(arrays + tuple(earlier))[: len(arrays)])


def shifted(array, axis, step):
    count = lax.axis_size(axis)
    return lax.ppermute(array, axis, [(i, (i + step) % count) for i in range(count)])


def swapped(array, axis, distance=1):
    count = lax.axis_size(axis)
    return lax.ppermute(array, axis, [(i, i ^ distance) for i in range(count)])


def pick(array, index, dimension=0):
    return lax.dynamic_index_in_dim(array, index, dimension, keepdims=False)


def paired(own, other, first, dimension):
    return jnp.where(
        first, jnp.stack([own, other], dimension), jnp.stack([other, own], dimension)
    )


def gather_axis(array, axis, dimension=0):
    count = lax.axis_size(axis)
    index = lax.axis_index(axis)
    if count == 2:
        return paired(array, swapped(array, axis), index == 0, dimension)
    shape = array.shape[:dimension] + (count,) + array.shape[dimension:]
    whole = jnp.zeros(shape, array.dtype)
    for step in range(count):
        piece = array if step == 0 else shifted(array, axis, step)
        whole = lax.dynamic_update_index_in_dim(
            whole, piece, (index + count - step) % count, dimension
        )
    return whole


class Chain:
    def __init__(self):
        self.done = []

    def swap(self, arrays, distances, before=(), during=()):
        before = tuple(a for some in before for a in some) + (self.done[-2] if len(self.done) > 1 else ())
        arrays = together(arrays, before)
        arrived = tuple(swapped(a, "to", d) for a, d in zip(arrays, distances))
        arrived = together(arrived, tuple(a for some in during for a in some))
        self.done.append(arrived)
        return arrived


def sum_rows(chain, first_kept, first_sent, second_kept, second_sent, before=(), during=()):
    count = lax.axis_size("to")
    index = lax.axis_index("to")
    rows, width = first_kept.shape
    shard = 2 * rows // count
    near, far = 1, count // 2
    while True:
        arrived = chain.swap((first_sent, second_sent), (near, far), before[:1], during[:1])
        before, during = before[1:], during[1:]
        near, far = 2 * near, far // 2
        yield
        if far < 1:
            return first_kept, arrived[0], second_kept, arrived[1]
        first = first_kept + arrived[0].astype(F32)
        second = second_kept + arrived[1].astype(F32)
        bit = lax.rem(index // near, 2)
        view = first.reshape(-1, 2, shard, width)
        first_sent = pick(view, 1 - bit, 1).astype(BF16).reshape(-1, width)
        first_kept = pick(view, bit, 1).reshape(-1, width)
        bit = lax.rem(index // far, 2)
        view = second.reshape(2, -1, width)
        second_sent = pick(view, 1 - bit).astype(BF16)
        second_kept = pick(view, bit)


def gather_rows(chain, shard, before=(), during=(), vector=None):
    before = tuple(before)
    count = lax.axis_size("to")
    index = lax.axis_index("to")
    rows = shard.shape[0]
    width = shard.shape[1] // 2
    first, second = shard[None, :, :width], shard[None, :, width:]
    far, near = count // 2, 1
    while far >= 1:
        arrays, distances = (first, second), (far, near)
        if vector is not None:
            arrays, distances = arrays + (vector,), distances + (near,)
        arrived = chain.swap(arrays, distances, before[:1], during[:1])
        before, during = before[1:], during[1:]
        if vector is not None:
            vector = vector + arrived[2]
        first = paired(first, arrived[0], lax.rem(index // far, 2) == 0, 1)
        second = paired(second, arrived[1], lax.rem(index // near, 2) == 0, 0)
        first = first.reshape(-1, rows, width)
        second = second.reshape(-1, rows, width)
        far, near = far // 2, 2 * near
        yield
    whole = jnp.concatenate([first.reshape(-1, width), second.reshape(-1, width)], axis=-1)
    return whole if vector is None else (whole, vector)


def gather_parts(chain, first, second, before=()):
    first, second = first[None], second[None]
    far, near = lax.axis_size("to") // 2, 1
    while True:
        arrived = chain.swap((first, second), (far, near), before[:1])
        before = before[1:]
        far, near = far // 2, 2 * near
        yield
        if far < 1:
            return first, arrived[0], second, arrived[1]
        first = jnp.concatenate([first, arrived[0]])
        second = jnp.concatenate([second, arrived[1]])


def gather_masks(count):
    orders = []
    for distances in (lambda i: count >> (i + 1), lambda i: 1 << i):
        masks = [0]
        for i in range(count.bit_length() - 1):
            masks += [mask | distances(i) for mask in masks]
        orders.append(masks)
    return orders


def run(*stages):
    results = [None] * len(stages)
    left = dict(enumerate(stages))
    while left:
        for index in list(left):
            try:
                next(left[index])
            except StopIteration as end:
                results[index] = end.value
                del left[index]
    return results


def sum_over(vector, axes):
    for axis in axes:
        distance = 1
        while distance < lax.axis_size(axis):
            vector = vector + swapped(vector, axis, distance)
            distance *= 2
    return vector


def over_pair(array, late=()):
    return jnp.concatenate([array, after(swapped(array, "ti"), *late)], axis=-1)


def over_blocks(array, late=()):
    count = lax.axis_size("bo")
    arrived = [after(shifted(array, "bo", step), *late) for step in range(1, count)]
    return jnp.stack([array] + arrived)


def over_cores(array):
    return array, swapped(array, "bi")


LOW, HIGH, INNER, FIRST, OUTER, PLACES = 0, 1, 2, 3, 4, 5


def mxu(left, right):
    return jnp.dot(left, right, preferred_element_type=F32)


def mxu_back(left, right):
    return lax.dot_general(left, right, (((1,), (1,)), ((), ())), preferred_element_type=F32)


def mxu_outer(left, right):
    return lax.dot_general(left, right, (((0,), (0,)), ((), ())), preferred_element_type=F32)


def columns(info, position, size):
    if info is None:
        return slice(position * size, (position + 1) * size)
    return pl.ds(pl.multiple_of(info[PLACES + position] * size, 128), size)


def project(info, rows_ref, *weights):
    blocks = [(ref, i) for ref in weights for i in range(ref.shape[0])]
    total = None
    for position, (ref, i) in enumerate(blocks):
        term = mxu(rows_ref[:, columns(info, position, ref.shape[1])], ref[i])
        total = term if total is None else total + term
    return total


def project_back(grads, position, *weights):
    blocks = [(ref, i) for ref in weights for i in range(ref.shape[0])]
    ref, i = blocks[position]
    return mxu_back(grads, ref[i])


def write_halves(info, counts, total_ref, outputs, place=0):
    first_kept, first_sent, second_kept, second_sent = outputs
    rows, width = total_ref.shape
    shard, middle = rows // counts, width // 2
    for j in range(counts // 2):
        for target, bit in ((first_kept, info[LOW]), (first_sent, 1 - info[LOW])):
            source = pl.ds(pl.multiple_of((2 * j + bit) * shard, shard), shard)
            target[j, place] = total_ref[source, :middle].astype(target.dtype)
        for target, bit in ((second_kept, info[HIGH]), (second_sent, 1 - info[HIGH])):
            source = pl.ds(pl.multiple_of((bit * (counts // 2) + j) * shard, shard), shard)
            target[j, place] = total_ref[source, middle:].astype(target.dtype)


def read_parts(info, counts, parts, target):
    rows, width = target.shape
    shard, middle = rows // counts, width // 2
    for side, masks in enumerate(gather_masks(counts)):
        for i, mask in enumerate(masks):
            ref = parts[2 * side + 2 * i // counts]
            place = pl.multiple_of(jnp.bitwise_xor(info[OUTER], mask) * shard, shard)
            columns_now = slice(side * middle, (side + 1) * middle)
            target[pl.ds(place, shard), columns_now] = ref[i % (counts // 2), 0]


def unit(values):
    return lax.rsqrt(jnp.mean(values * values, axis=-1, keepdims=True) + EPSILON)


def swap_halves(values):
    return pltpu.roll(values, values.shape[-1] // 2, 1)


def prepare_kernel(
    sizes,
    info,
    x_ref,
    gain_ref,
    query_gain_ref,
    key_gain_ref,
    cosine_ref,
    sine_ref,
    query_mine,
    query_theirs,
    kv_mine,
    kv_theirs,
    normal_ref,
    query_raw_ref,
    key_raw_ref,
    query_ref,
    kv_ref,
):
    head_dim, pair_heads, key_heads = sizes
    x = x_ref[0].astype(F32)
    normal_ref, query_raw_ref, key_raw_ref, query_ref, kv_ref = (
        ref.at[0] for ref in (normal_ref, query_raw_ref, key_raw_ref, query_ref, kv_ref)
    )
    normal_ref[...] = (x * unit(x) * gain_ref[...]).astype(BF16)
    cosine, sine = cosine_ref[...], sine_ref[...]

    def rotated(raw, gain):
        values = raw * unit(raw) * gain
        return (values * cosine + swap_halves(values) * sine).astype(BF16)

    query_raw = project(info, normal_ref, query_mine, query_theirs)
    query_raw_ref[...] = query_raw
    for head in range(query_raw.shape[1] // head_dim):
        part = slice(head * head_dim, (head + 1) * head_dim)
        query_ref[:, part] = rotated(query_raw[:, part], query_gain_ref[...])
    kv_raw = project(info, normal_ref, kv_mine, kv_theirs)
    for head in range(pair_heads):
        start = (2 * key_heads * (head // key_heads) + head % key_heads) * head_dim
        raw = kv_raw[:, start : start + head_dim]
        key_raw_ref[:, head * head_dim : (head + 1) * head_dim] = raw
        kv_ref[0, head] = rotated(raw, key_gain_ref[...])
        start += key_heads * head_dim
        kv_ref[1, head] = kv_raw[:, start : start + head_dim].astype(BF16)


def row_sums(parts):
    first_kept, first_arrived, second_kept, second_arrived = (ref[...] for ref in parts)
    return jnp.concatenate(
        [first_kept + first_arrived.astype(F32), second_kept + second_arrived.astype(F32)], axis=-1
    )


def norm_back(grad, values, gain):
    scale = unit(values)
    inner = grad * gain
    mean = jnp.mean(inner * values, axis=-1, keepdims=True)
    term = jnp.sum(grad * values * scale, axis=0, keepdims=True)
    return scale * inner - values * (scale * scale * scale * mean), term


def residual_kernel(x_ref, gain_ref, *refs):
    residual_ref, first_ref, second_ref = refs[4:]
    residual = x_ref[...].astype(F32) + row_sums(refs[:4])
    residual_ref[...] = residual
    normal = (residual * unit(residual) * gain_ref[...]).astype(BF16)
    middle = normal.shape[1] // 2
    first_ref[...] = normal[:, :middle]
    second_ref[...] = normal[:, middle:]


def residual_back_kernel(groups, residual_ref, grad_out_ref, gain_ref, *refs):
    layer_ref, grad_ref, first_ref, second_ref, term_ref = refs[4 * groups :]
    shard = residual_ref.shape[0] // groups
    middle = residual_ref.shape[1] // 2
    total = jnp.zeros(term_ref.shape, F32)
    for group in range(groups):
        place = slice(group * shard, (group + 1) * shard)
        sums = row_sums(refs[4 * group : 4 * group + 4])
        residual = residual_ref[place, :]
        layer_ref[place, :] = (residual + sums[shard:]).astype(BF16)
        grad, term = norm_back(sums[:shard], residual, gain_ref[...])
        grad += grad_out_ref[place, :].astype(F32)
        total += term
        grad_ref[place, :] = grad
        first_ref[place, :] = grad[:, :middle].astype(BF16)
        second_ref[place, :] = grad[:, middle:].astype(BF16)
    term_ref[...] = total


def hidden_kernel(x_ref, gain_ref, grad_residual_ref, *refs):
    hidden_ref, term_ref = refs[4:]
    grad, term = norm_back(row_sums(refs[:4]), x_ref[...].astype(F32), gain_ref[...])
    hidden_ref[...] = (grad_residual_ref[...] + grad).astype(BF16)
    term_ref[...] = term


def visible_scores(info, queries, keys, position, blocks, rows, scale):
    scores = mxu_back(queries, keys) * scale
    if position == 0:
        query_rows = lax.broadcasted_iota(jnp.int32, scores.shape, 0) % rows
        key_rows = lax.broadcasted_iota(jnp.int32, scores.shape, 1)
        return jnp.where(key_rows <= query_rows, scores, -jnp.inf)
    return jnp.where(info[PLACES + blocks + position] > 0, scores, -jnp.inf)


def attend_kernel(
    sizes,
    info,
    query_ref,
    kv_mine,
    kv_theirs,
    out_mine,
    out_theirs,
    attn_ref,
    log_ref,
    attended_ref,
    first_kept,
    first_sent,
    second_kept,
    second_sent,
    scores_ref,
    total_ref,
):
    head_dim, pair_heads, group, counts = sizes
    query_ref, attn_ref, log_ref, attended_ref = (
        ref.at[0] for ref in (query_ref, attn_ref, log_ref, attended_ref)
    )
    rows = query_ref.shape[0]
    half = kv_mine.shape[0]
    scale = head_dim ** (-0.5)
    lanes = lax.broadcasted_iota(jnp.int32, (rows, head_dim), 1)
    logs = jnp.zeros((rows, head_dim), F32)

    def key_value(which, position, head):
        ref = kv_mine if position < half else kv_theirs
        return ref[position % half, 0, which, head]

    for head in range(pair_heads):
        queries = jnp.concatenate(
            [
                query_ref[:, (head * group + i) * head_dim : (head * group + i + 1) * head_dim]
                for i in range(group)
            ]
        )
        top = None
        for position in range(2 * half):
            scores = visible_scores(
                info, queries, key_value(0, position, head), position, 2 * half, rows, scale
            )
            scores_ref[position] = scores
            block_top = jnp.max(scores, axis=-1, keepdims=True)
            top = block_top if top is None else jnp.maximum(top, block_top)
        total = jnp.zeros_like(top)
        weighted = jnp.zeros((group * rows, head_dim), F32)
        for position in range(2 * half):
            weights = jnp.exp(scores_ref[position] - top)
            total += jnp.sum(weights, axis=-1, keepdims=True)
            weighted += mxu(weights.astype(BF16), key_value(1, position, head))
        attn = weighted / total
        log_total = top + jnp.log(total)
        for i in range(group):
            index = head * group + i
            part = slice(index * head_dim, (index + 1) * head_dim)
            piece = attn[i * rows : (i + 1) * rows]
            attn_ref[:, part] = piece
            attended_ref[:, part] = piece.astype(BF16)
            logs = jnp.where(lanes == index, log_total[i * rows : (i + 1) * rows], logs)
    log_ref[...] = logs
    attended = attended_ref[...]
    for position in range(2 * half):
        total_ref[:, columns(info, position, out_mine.shape[1])] = project_back(
            attended, position, out_mine, out_theirs
        )
    write_halves(info, counts, total_ref, (first_kept, first_sent, second_kept, second_sent))


def feed_forward_kernel(
    counts,
    info,
    first_own,
    first_other,
    second_own,
    second_other,
    grad_ref,
    gate_ref,
    up_ref,
    down_ref,
    active_ref,
    grad_gate_ref,
    grad_up_ref,
    mid_ref,
    *outputs,
):
    grad_total, mlp_total = outputs[4:]
    step = pl.program_id(0)

    @pl.when(step == 0)
    def _():
        read_parts(info, counts, (first_own, first_other, second_own, second_other), mid_ref)

    blocks, size = gate_ref.shape[0], gate_ref.shape[1]
    gate = project(None, mid_ref, gate_ref)
    up = project(None, mid_ref, up_ref)
    grad = project(None, grad_ref.at[0], down_ref)
    slope = jax.nn.sigmoid(gate)
    silu = gate * slope
    active = (silu * up).astype(BF16)
    grad_gate = (grad * up * slope * (1.0 + gate * (1.0 - slope))).astype(BF16)
    grad_up = (grad * silu).astype(BF16)
    active_ref[...] = active
    grad_gate_ref[...] = grad_gate
    grad_up_ref[...] = grad_up

    def term(position):
        part = columns(None, position, size)
        grad_term = project_back(grad_gate, position, gate_ref) + project_back(
            grad_up, position, up_ref
        )
        return part, grad_term, project_back(active, position, down_ref)

    @pl.when(step == 0)
    def _():
        for position in range(blocks):
            part, grad_term, mlp_term = term(position)
            grad_total[:, part] = grad_term
            mlp_total[:, part] = mlp_term

    @pl.when(step > 0)
    def _():
        for position in range(blocks):
            part, grad_term, mlp_term = term(position)
            grad_total[:, part] += grad_term
            mlp_total[:, part] += mlp_term

    @pl.when(step == pl.num_programs(0) - 1)
    def _():
        write_halves(info, counts, grad_total, outputs[:4], 0)
        write_halves(info, counts, mlp_total, outputs[:4], 1)


def attend_back_kernel(
    sizes,
    info,
    first_own,
    first_other,
    second_own,
    second_other,
    out_mine,
    out_theirs,
    query_ref,
    kv_mine,
    kv_theirs,
    attn_ref,
    log_ref,
    branch_ref,
    grad_query_ref,
    kept_ref,
    sent_ref,
):
    head_dim, pair_heads, group, counts = sizes
    query_ref, attn_ref, log_ref, branch_ref, grad_query_ref = (
        ref.at[0] for ref in (query_ref, attn_ref, log_ref, branch_ref, grad_query_ref)
    )
    read_parts(info, counts, (first_own, first_other, second_own, second_other), branch_ref)
    rows = query_ref.shape[0]
    half = kv_mine.shape[0]
    scale = head_dim ** (-0.5)
    grad_attended = project(info, branch_ref, out_mine, out_theirs).astype(BF16)

    def key_value(which, position, head):
        ref = kv_mine if position < half else kv_theirs
        return ref[position % half, 0, which, head]

    for head in range(pair_heads):
        parts = [
            slice((head * group + i) * head_dim, (head * group + i + 1) * head_dim)
            for i in range(group)
        ]
        queries = jnp.concatenate([query_ref[:, part] for part in parts])
        grads = jnp.concatenate([grad_attended[:, part] for part in parts])
        attn = jnp.concatenate([attn_ref[:, part] for part in parts])
        logs = jnp.concatenate(
            [log_ref[:, head * group + i : head * group + i + 1] for i in range(group)]
        )
        row_dots = jnp.sum(grads.astype(F32) * attn, axis=-1, keepdims=True)
        grad_query = jnp.zeros((group * rows, head_dim), F32)
        for position in range(2 * half):
            keys = key_value(0, position, head)
            scores = visible_scores(info, queries, keys, position, 2 * half, rows, scale)
            probs = jnp.exp(scores - logs)
            grad_probs = mxu_back(grads, key_value(1, position, head))
            grad_scores = (probs * (grad_probs - row_dots) * scale).astype(BF16)
            grad_query += mxu(grad_scores, keys)
            target = kept_ref if position < half else sent_ref
            target[position % half, 0, 0, head] = mxu_outer(grad_scores, queries).astype(target.dtype)
            target[position % half, 0, 1, head] = mxu_outer(probs.astype(BF16), grads).astype(
                target.dtype
            )
        for i, part in enumerate(parts):
            grad_query_ref[:, part] = grad_query[i * rows : (i + 1) * rows]


def finish_kernel(
    sizes,
    info,
    grad_query_ref,
    query_raw_ref,
    key_raw_ref,
    shares_ref,
    query_gain_ref,
    key_gain_ref,
    cosine_ref,
    sine_ref,
    query_mine,
    query_theirs,
    kv_mine,
    kv_theirs,
    query_low_ref,
    kv_low_ref,
    gains_ref,
    first_kept,
    first_sent,
    second_kept,
    second_sent,
    total_ref,
):
    head_dim, pair_heads, key_heads, counts = sizes
    grad_query_ref, query_raw_ref, key_raw_ref, shares_ref, query_low_ref, kv_low_ref, gains_ref = (
        ref.at[0]
        for ref in (
            grad_query_ref,
            query_raw_ref,
            key_raw_ref,
            shares_ref,
            query_low_ref,
            kv_low_ref,
            gains_ref,
        )
    )
    cosine, sine = cosine_ref[...], sine_ref[...]

    def back(grad, raw, gain):
        grad = grad * cosine - swap_halves(grad) * sine
        scale = unit(raw)
        gain_term = jnp.sum(grad * raw * scale, axis=0, keepdims=True)
        inner = grad * gain
        mean = jnp.mean(inner * raw, axis=-1, keepdims=True)
        return (scale * inner - raw * (scale * scale * scale * mean)).astype(BF16), gain_term

    total = jnp.zeros((1, head_dim), F32)
    for head in range(query_raw_ref.shape[1] // head_dim):
        part = slice(head * head_dim, (head + 1) * head_dim)
        query_low_ref[:, part], term = back(
            grad_query_ref[:, part], query_raw_ref[:, part], query_gain_ref[...]
        )
        total += term
    gains_ref[0:1, :] = total
    total = jnp.zeros((1, head_dim), F32)
    for head in range(pair_heads):
        start = (2 * key_heads * (head // key_heads) + head % key_heads) * head_dim
        kv_low_ref[:, start : start + head_dim], term = back(
            shares_ref[0, head],
            key_raw_ref[:, head * head_dim : (head + 1) * head_dim],
            key_gain_ref[...],
        )
        total += term
        start += key_heads * head_dim
        kv_low_ref[:, start : start + head_dim] = shares_ref[1, head].astype(BF16)
    gains_ref[1:2, :] = total
    query_low, kv_low = query_low_ref[...], kv_low_ref[...]
    for position in range(2 * query_mine.shape[0]):
        total_ref[:, columns(info, position, query_mine.shape[1])] = project_back(
            query_low, position, query_mine, query_theirs
        ) + project_back(kv_low, position, kv_mine, kv_theirs)
    write_halves(info, counts, total_ref, (first_kept, first_sent, second_kept, second_sent))


def weight_kernel(counts, products, info, *refs):
    arrays, start = [], 0
    for count in counts:
        arrays.append(refs[start : start + count])
        start += count
    out_ref = refs[-1]

    def rows_of(members):
        flat = [ref[...].reshape(-1, ref.shape[-1]) for ref in members]
        return flat[0] if len(flat) == 1 else jnp.concatenate(flat)

    place = 0
    for left, rights in products:
        left_rows = rows_of(arrays[left])
        for right in rights:
            total = mxu_outer(left_rows, rows_of(arrays[right])).astype(BF16)
            if len(out_ref.shape) == 5:
                out_ref[0, 0, place] = total
                place += 1
            else:
                out_ref[0, 0, :, place : place + total.shape[1]] = total
                place += total.shape[1]


def whole_spec(dims):
    return pl.BlockSpec(dims, lambda i, info: (0,) * len(dims))


def group_spec(array, dimension=0):
    dims = array.shape[:dimension] + (1,) + array.shape[dimension + 1 :]
    rest = len(dims) - dimension - 1
    return pl.BlockSpec(dims, lambda g, info: (0,) * dimension + (g,) + (0,) * rest)


def plain_call(kernel, operands, outputs):
    moved = sum(a.size * a.dtype.itemsize for a in tuple(operands) + tuple(outputs))
    return pl.pallas_call(
        kernel,
        out_shape=tuple(outputs),
        compiler_params=pltpu.CompilerParams(vmem_limit_bytes=VMEM_LIMIT),
        cost_estimate=pl.CostEstimate(flops=0, bytes_accessed=moved, transcendentals=0),
    )(*operands)


def group_call(kernel, groups, info, operands, outputs, scratch=(), flops=0):
    moved = sum(a.size * a.dtype.itemsize for a, _ in tuple(operands) + tuple(outputs))
    return pl.pallas_call(
        kernel,
        out_shape=[a for a, _ in outputs],
        grid_spec=pltpu.PrefetchScalarGridSpec(
            num_scalar_prefetch=1,
            grid=(groups,),
            in_specs=[spec for _, spec in operands],
            out_specs=[spec for _, spec in outputs],
            scratch_shapes=list(scratch),
        ),
        compiler_params=pltpu.CompilerParams(vmem_limit_bytes=VMEM_LIMIT),
        cost_estimate=pl.CostEstimate(flops=flops, bytes_accessed=moved, transcendentals=0),
    )(info, *[a for a, _ in operands])


def shape(dims, dtype):
    return jax.ShapeDtypeStruct(dims, dtype)


def weight_blocks(info, lefts, rights, products, blocks, pair, stacked, in_order):
    width = lefts[0][0].shape[-1]
    size = width // blocks
    batch_rows = sum(a.shape[0] for a in lefts[0]) if lefts[0][0].ndim == 2 else None
    operands, specs = [], []
    for array in [a for members in lefts for a in members]:
        operands.append(array)
        if array.ndim == 2:
            spec = pl.BlockSpec((array.shape[0], size), lambda t, b, info: (0, b))
        elif array.shape[0] * array.shape[1] == batch_rows or batch_rows is None:
            spec = pl.BlockSpec(array.shape[:2] + (size,), lambda t, b, info: (0, 0, b))
        else:
            spec = pl.BlockSpec(
                (array.shape[0] // pair, array.shape[1], size),
                lambda t, b, info: (info[INNER], 0, b),
            )
        specs.append(spec)
    widths = []
    for members in rights:
        widths.append(members[0].shape[-1] // pair)
        for array in members:
            operands.append(array)
            dims = array.shape[:-1] + (array.shape[-1] // pair,)
            zeros = (0,) * (array.ndim - 1)
            specs.append(
                pl.BlockSpec(
                    dims,
                    lambda t, b, info, zeros=zeros: zeros
                    + (t if in_order else lax.rem(t + info[INNER], 2),),
                )
            )
    if stacked:
        dims = (pair, blocks, len(rights), size, widths[0])
        out_spec = pl.BlockSpec((1, 1) + dims[2:], lambda t, b, info: (t, b, 0, 0, 0))
    else:
        dims = (pair, blocks, size, sum(widths))
        out_spec = pl.BlockSpec((1, 1) + dims[2:], lambda t, b, info: (t, b, 0, 0))
    counts = [len(members) for members in tuple(lefts) + tuple(rights)]
    placed = [(left, [len(lefts) + right for right in columns_of]) for left, columns_of in products]
    rows = rights[0][0].size * len(rights[0]) // rights[0][0].shape[-1]
    flops = 2 * rows * width * pair * sum(widths)
    moved = 2 * pair * width * sum(widths)
    return pl.pallas_call(
        functools.partial(weight_kernel, counts, placed),
        out_shape=shape(dims, BF16),
        grid_spec=pltpu.PrefetchScalarGridSpec(
            num_scalar_prefetch=1,
            grid=(pair, blocks),
            in_specs=specs,
            out_specs=out_spec,
        ),
        compiler_params=pltpu.CompilerParams(vmem_limit_bytes=VMEM_LIMIT),
        cost_estimate=pl.CostEstimate(flops=flops, bytes_accessed=moved, transcendentals=0),
    )(info, *operands)


def local(
    hidden_in,
    out_grad,
    norm_in,
    w_query,
    key_weight,
    value_weight,
    w_out,
    query_gain,
    key_gain,
    norm_mid,
    w_gate,
    w_up,
    w_down,
):
    block_outers = lax.axis_size("bo")
    blocks = block_outers * lax.axis_size("bi")
    block_outer = lax.axis_index("bo")
    block_inner = lax.axis_index("bi")
    block = block_outer * lax.axis_size("bi") + block_inner
    outer = lax.axis_index("to")
    inner = lax.axis_index("ti")
    pair = lax.axis_size("ti")
    counts = lax.axis_size("to")
    batch, rows, width = hidden_in.shape
    head_dim = query_gain.shape[0] * blocks
    query_width = w_query.shape[1]
    key_width = key_weight.shape[1]
    hidden_units = w_gate.shape[1]
    key_heads = key_width // head_dim
    query_heads = query_width * pair // head_dim
    pair_heads = key_heads * pair
    group_size = query_heads // pair_heads
    shard_rows = rows // counts

    query_half = over_pair(w_query)
    kv_half = over_blocks(jnp.concatenate([key_weight, value_weight], axis=1))
    query_most = over_blocks(query_half)
    kv_most = over_pair(kv_half)
    query_full = over_cores(query_most)
    kv_full = over_cores(kv_most)
    out_half = over_blocks(after(w_out.T, query_half))
    mlp_own = jnp.concatenate([w_gate, w_up, w_down.T], axis=1)

    own_gains = jnp.concatenate([norm_in, norm_mid, query_gain, key_gain])[None]
    own_gains = after(own_gains, kv_half)
    all_gains = gather_axis(gather_axis(own_gains, "bo"), "bi", 1)
    all_gains = all_gains.reshape(blocks, -1).astype(F32)
    part = norm_in.shape[0]
    gain_in = all_gains[:, :part].reshape(-1)
    gain_mid = all_gains[:, part : 2 * part].reshape(-1)
    head_part = query_gain.shape[0]
    gain_query = all_gains[:, 2 * part : 2 * part + head_part].reshape(1, -1)
    gain_key = all_gains[:, 2 * part + head_part :].reshape(1, -1)

    positions = block * rows + jnp.arange(rows, dtype=jnp.int32)
    cosine, sine = rotation_tables(positions, head_dim)
    block_ids = []
    for side in range(2):
        side_inner = block_inner if side == 0 else 1 - block_inner
        for step in range(block_outers):
            owner = lax.rem(block_outer + block_outers - step, block_outers)
            block_ids.append(owner * 2 + side_inner)
    groups = batch // pair
    first_sequence = inner * groups
    info = jnp.stack(
        [lax.rem(outer, 2), outer // (counts // 2), inner, first_sequence, outer]
        + block_ids
        + [(b < block).astype(jnp.int32) for b in block_ids]
    ).astype(jnp.int32)

    chain = Chain()
    all_heads = query_heads * head_dim
    all_keys = pair_heads * head_dim
    kv_dims = (groups, 2, pair_heads, rows, head_dim)
    side_dims = (block_outers,) + kv_dims
    half_dims = (counts // 2, groups, shard_rows, width // 2)
    whole_rows = pltpu.VMEM((rows, width), F32)

    def by_group(dims, dtype, dimension=0):
        array = shape(dims, dtype)
        return array, group_spec(array, dimension)

    def per_group(*arrays):
        return tuple((a, group_spec(a)) for a in arrays)

    def per_second(*arrays):
        return tuple((a, group_spec(a, 1)) for a in arrays)

    def shared(*arrays):
        return tuple((a, whole_spec(a.shape)) for a in arrays)

    halves = (by_group(half_dims, F32, 1), by_group(half_dims, BF16, 1)) * 2

    def flat(parts):
        return [part.reshape(-1, part.shape[-1]) for part in parts]

    def own_sequences(array):
        return (array, pl.BlockSpec((1, rows, width), lambda g, info: (info[FIRST] + g, 0, 0)))

    normal_in, query_raw, key_raw, query_rows, kv_rows = group_call(
        functools.partial(prepare_kernel, (head_dim, pair_heads, key_heads)),
        groups,
        info,
        (own_sequences(hidden_in),)
        + shared(after(gain_in[None], out_half), gain_query, gain_key, cosine, sine)
        + shared(*query_full, *kv_full),
        (
            by_group((groups, rows, width), BF16),
            by_group((groups, rows, all_heads), F32),
            by_group((groups, rows, all_keys), F32),
            by_group((groups, rows, all_heads), BF16),
            by_group(kv_dims, BF16),
        ),
        flops=2 * groups * rows * width * (all_heads + 2 * all_keys),
    )
    mlp_own = with_layout_constraint(after(mlp_own, query_rows), Layout((0, 1)))
    mlp_weights = lax.all_gather(mlp_own, ("ti", "bo", "bi"), axis=0)
    kv_blocks = over_blocks(kv_rows)
    key_value = over_cores(kv_blocks)
    out_full = over_cores(over_pair(out_half, (kv_blocks,)))
    attn, log_total, attended, *out_parts = group_call(
        functools.partial(attend_kernel, (head_dim, pair_heads, group_size, counts)),
        groups,
        info,
        per_group(query_rows) + per_second(*key_value) + shared(*out_full),
        (
            by_group((groups, rows, all_heads), F32),
            by_group((groups, rows, head_dim), F32),
            by_group((groups, rows, all_heads), BF16),
        )
        + halves,
        scratch=[pltpu.VMEM((blocks, group_size * rows, rows), F32), whole_rows],
        flops=2 * groups * rows * all_heads * (width + 4 * blocks * rows),
    )

    def own_shard(array):
        starts = (first_sequence, outer * shard_rows, 0)
        part = lax.dynamic_slice(array, starts, (groups, shard_rows, width))
        return part.reshape(-1, width)

    x_shard = own_shard(hidden_in)
    grad_out_shard = own_shard(out_grad)
    shard_dims = (groups * shard_rows, width)
    half_shard = shape((groups * shard_rows, width // 2), BF16)
    (sums,) = run(sum_rows(chain, *flat(out_parts)))
    residual, *normal_mid = plain_call(
        residual_kernel,
        (x_shard, gain_mid[None]) + sums,
        (shape(shard_dims, F32), half_shard, half_shard),
    )
    normal_mid = [half.reshape(groups, shard_rows, -1) for half in normal_mid]
    mid_parts = []
    for group in range(groups):
        mid_parts += run(gather_parts(chain, *(half[group] for half in normal_mid)))

    chunks = pair * hidden_units // HIDDEN_CHUNK
    steps = hidden_units // HIDDEN_CHUNK
    weight_dims = (blocks, width // blocks, HIDDEN_CHUNK)

    def weight_spec(place):
        return pl.BlockSpec(
            weight_dims, lambda i, info: (i // steps, 0, place * steps + lax.rem(i, steps))
        )

    piece = pl.BlockSpec((rows, HIDDEN_CHUNK), lambda i, info: (0, i))
    hidden_shape = shape((rows, pair * hidden_units), BF16)
    one_dims = (counts // 2, 1, shard_rows, width // 2)
    two_dims = (counts // 2, 2, shard_rows, width // 2)
    two_halves = (shape(two_dims, F32), shape(two_dims, BF16)) * 2
    mid, active, grad_gate, grad_up, mlp_parts = [], [], [], [], []
    for group in range(groups):
        parts = [part.reshape(one_dims) for part in mid_parts[group]]
        sequence = pl.BlockSpec(
            (1, rows, width), lambda i, info, group=group: (info[FIRST] + group, 0, 0)
        )
        results = pl.pallas_call(
            functools.partial(feed_forward_kernel, counts),
            out_shape=(hidden_shape,) * 3 + (shape((rows, width), BF16),) + two_halves,
            grid_spec=pltpu.PrefetchScalarGridSpec(
                num_scalar_prefetch=1,
                grid=(chunks,),
                in_specs=[whole_spec(one_dims)] * 4 + [sequence] + [weight_spec(i) for i in range(3)],
                out_specs=(piece,) * 3 + (whole_spec((rows, width)),) + (whole_spec(two_dims),) * 4,
                scratch_shapes=[whole_rows] * 2,
            ),
            compiler_params=pltpu.CompilerParams(vmem_limit_bytes=VMEM_LIMIT),
            cost_estimate=pl.CostEstimate(
                flops=12 * rows * width * pair * hidden_units,
                bytes_accessed=6 * width * pair * hidden_units,
                transcendentals=rows * pair * hidden_units,
            ),
        )(info, *parts, out_grad, mlp_weights, mlp_weights, mlp_weights)
        active.append(results[0])
        grad_gate.append(results[1])
        grad_up.append(results[2])
        mid.append(results[3])
        mlp_parts.append(results[4:])

    both_sums = []
    first_arrived = ()
    for group in range(groups - 1):
        mark = len(chain.done)
        both_sums += run(sum_rows(chain, *flat(mlp_parts[group]), during=((active[-1],),)))
        first_arrived = chain.done[mark]
    mlp_terms = weight_blocks(
        after(info, *first_arrived),
        (mid, [out_grad]),
        (grad_gate, grad_up, active),
        [(0, [0, 1]), (1, [2])],
        blocks,
        pair,
        True,
        True,
    )
    both_sums += run(sum_rows(chain, *flat(mlp_parts[-1]), during=((mlp_terms,),)))
    last_arrived = chain.done[-1]
    layer_shard, grad_residual, *branch_halves, gain_mid_term = plain_call(
        functools.partial(residual_back_kernel, groups),
        (residual, grad_out_shard, gain_mid[None]) + tuple(a for sums in both_sums for a in sums),
        (
            shape(shard_dims, BF16),
            shape(shard_dims, F32),
            half_shard,
            half_shard,
            shape((1, width), F32),
        ),
    )

    half_groups = groups // 2

    def in_order(own, arrived):
        return paired(own, arrived, inner == 0, 0)

    layer_shard = layer_shard.reshape(groups, shard_rows, width)
    late = layer_shard[half_groups:].reshape(-1, width)
    late_arrived = swapped(late, "ti")
    late = in_order(late, late_arrived).reshape(-1, width)
    early_rows = half_groups * shard_rows
    layer_rows = jnp.concatenate([layer_shard[:half_groups].reshape(-1, width), late])
    (branch_parts,) = run(
        gather_parts(chain, *branch_halves, ((), (late_arrived,)))
    )
    branch_parts = [part.reshape(half_dims) for part in branch_parts]
    branch, grad_query, kv_kept, kv_sent = group_call(
        functools.partial(attend_back_kernel, (head_dim, pair_heads, group_size, counts)),
        groups,
        info,
        per_second(*branch_parts)
        + shared(*out_full)
        + per_group(query_rows)
        + per_second(*key_value)
        + per_group(attn, log_total),
        (
            by_group((groups, rows, width), BF16),
            by_group((groups, rows, all_heads), F32),
            by_group(side_dims, F32, 1),
            by_group(side_dims, BF16, 1),
        ),
        flops=2 * groups * rows * all_heads * (width + 10 * blocks * rows),
    )

    kv_arrived = swapped(kv_sent, "bi")
    mine = kv_kept + kv_arrived.astype(F32)
    low = mine.astype(BF16)

    layer_chain = Chain()
    layer_stage = gather_rows(layer_chain, layer_rows, ((kv_arrived,),))
    next(layer_stage)
    layer_first = layer_chain.done[0]
    shares = mine[0]
    for step in range(1, block_outers):
        arrived = shifted(low[step], "bo", block_outers - step)
        shares += after(arrived, *layer_first).astype(F32)
    (layer_whole,) = run(layer_stage)
    layer_second = layer_chain.done[1:]
    layer_whole = layer_whole.reshape(counts, -1, width)
    layer_early = layer_whole[:, :early_rows]
    layer_arrived = swapped(layer_early, "ti")

    grad_query_low, grad_kv_low, gain_terms, *in_parts = group_call(
        functools.partial(finish_kernel, (head_dim, pair_heads, key_heads, counts)),
        groups,
        info,
        per_group(grad_query, query_raw, key_raw, shares)
        + shared(gain_query, gain_key, cosine, sine, *query_full, *kv_full),
        (
            by_group((groups, rows, all_heads), BF16),
            by_group((groups, rows, 2 * all_keys), BF16),
            by_group((groups, 2, head_dim), F32),
        )
        + halves,
        scratch=[whole_rows],
        flops=2 * groups * rows * width * (all_heads + 2 * all_keys),
    )
    attn_terms = weight_blocks(
        info,
        ([normal_in], [branch]),
        ([grad_query_low], [grad_kv_low], [attended]),
        [(0, [0, 1]), (1, [2])],
        blocks,
        pair,
        False,
        False,
    )

    in_parts = flat(in_parts)
    during = ((attn_terms,), (layer_arrived,))
    (sums,) = run(sum_rows(chain, *in_parts, before=layer_second, during=during))
    sum_arrived = chain.done[-1]
    hidden_shard, gain_in_term = plain_call(
        hidden_kernel,
        (x_shard, gain_in[None], grad_residual) + sums,
        (shape(shard_dims, BF16), shape((1, width), F32)),
    )
    hidden_shard = hidden_shard.reshape(groups, shard_rows, width)

    def weight_sum(terms):
        flat = terms.reshape((-1,) + terms.shape[-1:])
        raw = lax.psum_scatter(flat, ("ti", "bo", "bi"), scatter_dimension=0, tiled=True)
        share = with_layout_constraint(raw, Layout((0, 1)))
        return share.astype(F32).reshape(terms.shape[2:]), raw

    share_mlp, mlp_raw = weight_sum(after(mlp_terms, *last_arrived))
    share_attn, _ = weight_sum(after(attn_terms, mlp_raw, *sum_arrived))
    vectors = jnp.concatenate(
        [gain_in_term[0], gain_mid_term[0], gain_terms.sum(0).reshape(-1)]
    )
    hidden_late = hidden_shard[half_groups:].reshape(-1, width)
    hidden_arrived = swapped(hidden_late, "ti")
    vectors = vectors[None]
    vector_arrived = swapped(vectors, "ti")
    hidden_early = hidden_shard[:half_groups].reshape(-1, width)
    (hidden_early,) = run(gather_rows(chain, hidden_early, ((), (hidden_arrived,))))
    hidden_early_arrived = swapped(hidden_early, "ti")
    vectors = sum_over(vectors + after(vector_arrived, *chain.done[-2]), BLOCKS)
    mlp_grads = (share_mlp[0], share_mlp[1], share_mlp[2].T)
    hidden_late = in_order(hidden_late, hidden_arrived).reshape(-1, width)
    hidden_early_arrived = after(hidden_early_arrived, *mlp_grads)
    during = ((), (hidden_early_arrived,))
    ((hidden_late, vectors),) = run(
        gather_rows(chain, hidden_late, during=during, vector=vectors)
    )
    vectors = vectors[0]
    kv_start = query_width + 2 * key_width
    attn_grads = (
        share_attn[:, :query_width],
        share_attn[:, query_width : query_width + key_width],
        share_attn[:, query_width + key_width : kv_start],
        share_attn[:, kv_start:].T,
    )

    def assembled(early, arrived, late):
        late = late.reshape(counts, pair, groups - half_groups, shard_rows, width)
        late = late.transpose(1, 2, 0, 3, 4).reshape(pair, -1, rows, width)
        early = in_order(early, arrived).reshape(pair, counts, half_groups, shard_rows, width)
        early = early.transpose(0, 2, 1, 3, 4).reshape(pair, -1, rows, width)
        return jnp.concatenate([early, late], axis=1).reshape(batch, rows, width)

    layer_out = assembled(layer_early, layer_arrived, layer_whole[:, early_rows:])
    hidden_early_arrived = after(hidden_early_arrived, layer_out)
    grad_hidden = assembled(hidden_early, hidden_early_arrived, hidden_late)

    def vector_share(first, size):
        return lax.dynamic_slice_in_dim(vectors, first + block * (size // blocks), size // blocks)

    return (
        layer_out,
        grad_hidden,
        vector_share(0, width),
        *attn_grads,
        vector_share(2 * width, head_dim),
        vector_share(2 * width + head_dim, head_dim),
        vector_share(width, width),
        *mlp_grads,
    )


def solution(mesh):
    block_count, tensor_count = mesh.devices.shape
    split = Mesh(
        mesh.devices.reshape(block_count // 2, 2, tensor_count // 2, 2), BLOCKS + TENSORS
    )
    row_weight = P(BLOCKS, TENSORS)
    column_weight = P(TENSORS, BLOCKS)
    tokens = P(None, BLOCKS, None)
    vector = P(BLOCKS)
    weights = (
        vector,
        row_weight,
        row_weight,
        row_weight,
        column_weight,
        vector,
        vector,
        vector,
        row_weight,
        row_weight,
        column_weight,
    )
    return jax.shard_map(
        local,
        mesh=split,
        in_specs=(tokens, tokens) + weights,
        out_specs=(tokens, tokens) + weights,
        check_vma=False,
    )
```
